768 devices in a mesh: gx: 12 (over z_lo, x), gy: 64 (over z_hi, y, core).
Axes of the slice: x: 4, y: 8, z: 12 (z_hi: 4, z_lo: 3; z = z_hi * 3 + z_lo), core: 2. Of those that a mesh axis runs over, the one named last changes fastest.
Arguments:
- density: float32 [192, 512, 256], P('gx', 'gy'), may hold values from 0.05 to 1
- force: float32 [3, 192, 512, 256], P(None, 'gx', 'gy'), may hold values from -40 to 40
- brick_ids: int32 [12, 64, 512], P('gx', 'gy'), may hold values from 0 to 512, as said below
- offsets: int32 [14, 3], replicated, may hold values from -1 to 1, as said below
Outputs:
- displacement: float32 [3, 192, 512, 256], P(None, 'gx', 'gy')
- sensitivity: float32 [192, 512, 256], P('gx', 'gy')
The draws below stay inside these ranges and needn't reach their ends.
Inputs may be any that keep to these rules, and one draw needn't show every extreme that they name: `brick_ids`: each device's row lists the numbers of the solid bricks of its block, distinct and ascending, followed by the padding value 512 in the remaining slots; at least half of a block's bricks are solid and at least one slot is padding. `offsets`: 14 distinct rows (dx, dy, dz); the first row is (0, 0, 0).
All inputs are finite; a program needn't handle non-finite values.
Results may differ from the reference program's by a relative error of at most 0.0065.
Values sent between devices are 32-bit elements; how exact they have to be, the bound alone decides.
No kernel may reach another device: no remote copies, remote signals or barrier semaphores. Data moves between devices by JAX's collectives and lax.ppermute only.
A program may use at most 32 MiB of HBM per device.

```python
import jax
import jax.numpy as jnp
import numpy as np
from jax import lax

CX = 16
CY = 8
CZ = 256
ITERS = 2
NOFF = 14
DEV_X = 12
DEV_Y = 64
BPD = 512
NX = 192
NY = 512
NZ = 256


def draw_brick_ids(key, part):
    key = jax.random.fold_in(key, 11)
    count_key, rank_key = jax.random.split(key)
    blocks = DEV_X * DEV_Y
    counts = jax.random.randint(count_key, (blocks, 1), BPD // 2, BPD)
    ranks = jax.vmap(lambda single: jax.random.permutation(single, BPD))(jax.random.split(rank_key, blocks))
    listed = jnp.where(ranks < counts, jnp.arange(BPD, dtype=jnp.int32)[None, :], BPD)
    return jnp.sort(listed, axis=1).astype(jnp.int32).reshape(DEV_X, DEV_Y, BPD)


def draw_offsets(key, part):
    key = jax.random.fold_in(key, 23)
    picked = jax.random.permutation(key, 26)[:NOFF - 1].astype(jnp.int32)
    picked = jnp.where(picked >= 13, picked + 1, picked)
    chosen = jnp.concatenate([jnp.full((1,), 13, jnp.int32), picked])
    return jnp.stack([chosen // 9 - 1, chosen // 3 % 3 - 1, chosen % 3 - 1], axis=1).astype(jnp.int32)


def draw_force(key, part):
    key = jax.random.fold_in(key, 37)
    base_key = jax.random.fold_in(key, 0)
    ramp_x = 0.6 + 1.2 * jnp.arange(NX, dtype=jnp.float32) / max(NX - 1, 1)
    ramp_y = 0.6 + 1.2 * jnp.arange(NY, dtype=jnp.float32) / max(NY - 1, 1)
    base = jnp.clip(jax.random.normal(base_key, (3, NX, NY, NZ), jnp.float32), -5.0, 5.0)
    load = base * ramp_x[None, :, None, None] * ramp_y[None, None, :, None]
    return load.astype(jnp.float32)


def levels(own_key, extent, pieces, least, largest):
    factor_of, own = 1.0, jax.random.fold_in(own_key, 6)
    for axis_at, parts in pieces:
        heights = jnp.exp(jax.random.uniform(jax.random.fold_in(own, axis_at), (parts,), jnp.float32, least / len(pieces), largest / len(pieces)))
        factor_of = factor_of * jnp.repeat(heights, extent[axis_at] // parts).reshape([-1 if axis == axis_at else 1 for axis in range(len(extent))])
    return factor_of


def setup_inputs(seed: int = 0) -> dict:
    keys = jax.random.split(jax.random.key(seed), 5)
    return {
        "density": jnp.clip(0.05 + 0.95 * jax.random.uniform(keys[0], (NX, NY, NZ), jnp.float32) ** levels(keys[0], (NX, NY, NZ), ((0, 12), (1, 64)), -0.2, 0.2), 0.05, 1.0),
        "force": draw_force(jax.random.fold_in(keys[4], 71), 0),
        "brick_ids": draw_brick_ids(jax.random.fold_in(keys[4], 71), 0),
        "offsets": draw_offsets(jax.random.fold_in(keys[4], 71), 0),
    }


CUBE = np.array([[i // 9 - 1, i // 3 % 3 - 1, i % 3 - 1] for i in range(27)], dtype=np.int32)
REACH = np.sqrt((CUBE ** 2).sum(axis=1)).astype(np.float32)
GAINS = np.where(np.eye(3) > 0, 2.0, 1.0).astype(np.float32)
EMIN = 0.001
RADIUS = 2.0

def stencil_weights(offsets):
    match = jnp.all(offsets[None, :, :] == jnp.asarray(CUBE)[:, None, :], axis=2)
    chosen = jnp.any(match, axis=1)
    return jnp.where(chosen, RADIUS - jnp.asarray(REACH), 0.0).astype(jnp.float32)

def apply_filter(padded, weights, sign):
    sizes = [padded.shape[a] - 2 for a in range(3)]
    total = jnp.zeros(sizes, padded.dtype)
    for index in range(27):
        begin = [1 + int(CUBE[index, a]) * sign for a in range(3)]
        piece = padded[begin[0]:begin[0] + sizes[0], begin[1]:begin[1] + sizes[1], begin[2]:begin[2] + sizes[2]]
        total = total + weights[index] * piece
    return total

def interior(padded):
    return padded[..., 1:-1, 1:-1, 1:-1]

def neighbours(padded):
    return [(padded[..., 2:, 1:-1, 1:-1], padded[..., :-2, 1:-1, 1:-1]), (padded[..., 1:-1, 2:, 1:-1], padded[..., 1:-1, :-2, 1:-1]), (padded[..., 1:-1, 1:-1, 2:], padded[..., 1:-1, 1:-1, :-2])]

def face_couplings(stiff_pad):
    centre = interior(stiff_pad)
    return [(0.5 * (centre + upper), 0.5 * (centre + lower)) for upper, lower in neighbours(stiff_pad)]

def apply_operator(padded, couplings):
    centre = interior(padded)
    total = jnp.zeros_like(centre)
    for index, pair in enumerate(neighbours(padded)):
        gain = jnp.asarray(GAINS[:, index]).reshape(3, 1, 1, 1)
        upper_c, lower_c = couplings[index]
        total = total + gain * (upper_c * (centre - pair[0]) + lower_c * (centre - pair[1]))
    return total

def strain_energy(padded):
    centre = interior(padded)
    total = jnp.zeros_like(centre)
    for index, pair in enumerate(neighbours(padded)):
        gain = jnp.asarray(GAINS[:, index]).reshape(3, 1, 1, 1)
        total = total + gain * ((centre - pair[0]) ** 2 + (centre - pair[1]) ** 2)
    return 0.5 * lax.optimization_barrier(jnp.sum(total, axis=0))

def brick_mask(brick_ids):
    blocks = DEV_X * DEV_Y
    listed = brick_ids.reshape(blocks, BPD)
    block_rows = jnp.arange(blocks, dtype=jnp.int32)[:, None]
    flags = jnp.zeros((blocks, BPD + 1), jnp.float32).at[block_rows, listed].set(1.0)[:, :BPD]
    flags = flags.reshape(DEV_X, DEV_Y, CX // 4, 1, CY // 4, 1, CZ // 4, 1)
    cells = jnp.broadcast_to(flags, (DEV_X, DEV_Y, CX // 4, 4, CY // 4, 4, CZ // 4, 4))
    cells = cells.reshape(DEV_X, DEV_Y, CX, CY, CZ)
    return cells.transpose(0, 2, 1, 3, 4).reshape(NX, NY, NZ)

def reference(density, force, brick_ids, offsets):
    weights = stencil_weights(offsets)
    solid_mask = brick_mask(brick_ids)
    weight_total = apply_filter(jnp.pad(jnp.ones_like(density), 1), weights, 1)
    smooth = apply_filter(jnp.pad(density, 1), weights, 1) / weight_total
    stiffness = EMIN + solid_mask * smooth ** 3 * (1.0 - EMIN)
    couplings = face_couplings(jnp.pad(stiffness, 1))
    vector_pad = ((0, 0), (1, 1), (1, 1), (1, 1))
    motion = jnp.zeros_like(force)
    residual = force
    direction = force
    norm_now = jnp.sum(residual * residual)
    for step in range(ITERS):
        image = apply_operator(jnp.pad(direction, vector_pad), couplings)
        step_size = norm_now / jnp.sum(direction * image)
        motion = motion + step_size * direction
        residual = residual - step_size * image
        if step + 1 < ITERS:
            norm_next = jnp.sum(residual * residual)
            direction = residual + norm_next / norm_now * direction
            norm_now = norm_next
    energy = strain_energy(jnp.pad(motion, vector_pad))
    share_term = -3.0 * (1.0 - EMIN) * solid_mask * smooth ** 2 * energy / weight_total
    sensitivity = apply_filter(jnp.pad(share_term, 1), weights, -1)
    return (motion, sensitivity)
```

```python
import functools

import jax
import jax.numpy as jnp
import numpy as np
from jax import lax
from jax.experimental import pallas as pl
from jax.experimental.pallas import tpu as pltpu
from jax.sharding import Mesh
from jax.sharding import PartitionSpec as P

EMIN = 0.001
RADIUS = 2.0
REACH = [float(np.float32(RADIUS) - np.float32(np.sqrt(np.float32(s)))) for s in range(4)]

CX, CY, CZ = 16, 8, 256
NX, NY = 192, 512
ROWS = 16
F32 = jnp.float32


def sub_iota(rows):
    return lax.broadcasted_iota(jnp.int32, (rows, CZ), 0)


def lane_iota(rows):
    return lax.broadcasted_iota(jnp.int32, (rows, CZ), 1)


def roll(v, shift, axis):
    return pltpu.roll(v, shift % v.shape[axis], axis)


def yp(v):
    return roll(v, -1, 0)


def ym(v):
    return roll(v, 1, 0)


def zp(v, lane, fill=0.0):
    return jnp.where(lane == CZ - 1, fill, roll(v, -1, 1))


def zm(v, lane, fill=0.0):
    return jnp.where(lane == 0, fill, roll(v, 1, 1))


def pack_y_kernel(den_ref, f_ref, ids_ref, lo_ref, hi_ref, m_ref):
    ids = ids_ref[...]
    row = lax.shift_right_logical(ids, 6)
    col = lax.bitwise_and(ids, 63)
    p = (lax.broadcasted_iota(jnp.int32, (8, 512), 0) == row).astype(jnp.bfloat16)
    q = (
        lax.shift_right_logical(lax.broadcasted_iota(jnp.int32, (CZ, 512), 0), 2) == col
    ).astype(jnp.bfloat16)
    m_ref[...] = lax.dot_general(p, q, (((1,), (1,)), ((), ())), preferred_element_type=F32)
    sub = sub_iota(8)
    low = sub < 4

    def step(x, _):
        base = lax.shift_right_logical(x, 2) * 2
        den, f0, f1, f2 = den_ref[x], f_ref[0, x], f_ref[1, x], f_ref[2, x]
        f0r, f2r = roll(f0, 4, 0), roll(f2, 4, 0)
        lo_ref[x, 0:8] = jnp.where(sub == 7, m_ref[pl.ds(base, 1)], jnp.where(low, den, f0r))
        lo_ref[x, 8:16] = jnp.where(low, f1, f2r)
        hi_ref[x, 0:8] = jnp.where(sub == 0, m_ref[pl.ds(base + 1, 1)], jnp.where(low, f0r, den))
        hi_ref[x, 8:16] = jnp.where(low, f2r, f1)
        return 0

    lax.fori_loop(0, CX, step, 0, unroll=2)


def pack_x_kernel(den_ref, f_ref, m_ref, up_ref, dn_ref, bd_ref, bf_ref, lo_ref, hi_ref):
    sub = sub_iota(8)
    low = sub < 4

    def step(x, _):
        base = lax.shift_right_logical(x, 2) * 2
        u0, u1 = up_ref[x, 0:8], up_ref[x, 8:16]
        d0, d1 = dn_ref[x, 0:8], dn_ref[x, 8:16]
        bd_ref[x] = jnp.where(low, u0, d0)
        bf_ref[0, x] = roll(jnp.where(low, d0, u0), 4, 0)
        f1 = jnp.where(low, u1, d1)
        f1 = jnp.where(sub == 3, m_ref[pl.ds(base, 1)], f1)
        bf_ref[1, x] = jnp.where(sub == 4, m_ref[pl.ds(base + 1, 1)], f1)
        bf_ref[2, x] = roll(jnp.where(low, d1, u1), 4, 0)
        return 0

    lax.fori_loop(0, CX, step, 0, unroll=2)
    for slab, dx0, fx0 in ((lo_ref, 0, 0), (hi_ref, 12, 13)):
        for j in range(4):
            slab[j, 0:8] = den_ref[dx0 + j]
            slab[j, 8:16] = bd_ref[dx0 + j]
        for c in range(3):
            for j in range(3):
                slab[4 + 3 * c + j, 0:8] = f_ref[c, fx0 + j]
                slab[4 + 3 * c + j, 8:16] = bf_ref[c, fx0 + j]


def load_weights(off_ref, w_ref):
    for i in range(27):
        w_ref[i] = jnp.float32(0.0)
    for j in range(off_ref.shape[0]):
        dx, dy, dz = off_ref[j, 0], off_ref[j, 1], off_ref[j, 2]
        s = dx * dx + dy * dy + dz * dz
        w = jnp.where(
            s == 0,
            jnp.float32(REACH[0]),
            jnp.where(
                s == 1, jnp.float32(REACH[1]), jnp.where(s == 2, jnp.float32(REACH[2]), jnp.float32(REACH[3]))
            ),
        )
        w_ref[(dx + 1) * 9 + (dy + 1) * 3 + dz + 1] = w


def filter_plane(planes, w_ref, lane, sign):
    out = None
    for dz in (-1, 0, 1):
        acc = None
        for dy in (-1, 0, 1):
            t = None
            for dx in (-1, 0, 1):
                w = w_ref[(sign * dx + 1) * 9 + (sign * dy + 1) * 3 + sign * dz + 1]
                term = planes[dx + 1] * w
                t = term if t is None else t + term
            if dy == 1:
                t = yp(t)
            elif dy == -1:
                t = ym(t)
            acc = t if acc is None else acc + t
        if dz == 1:
            acc = zp(acc, lane)
        elif dz == -1:
            acc = zm(acc, lane)
        out = acc if out is None else out + acc
    return out


def image_plane(load, s_m, s_0, s_p, lane):
    px, mx = 0.5 * (s_0 + s_p), 0.5 * (s_0 + s_m)
    py = 0.5 * (s_0 + yp(s_0))
    pz = 0.5 * (s_0 + zp(s_0, lane))
    half = -0.5 * s_0
    outs = []
    for c in range(3):
        v = load(c, 0)
        fx = px * (v - load(c, 1)) + mx * (v - load(c, -1))
        fy = py * (v - yp(v))
        fy = fy - ym(fy)
        fz = pz * (v - zp(v, lane))
        fz = fz - zm(fz, lane, half * v)
        outs.append(fx + fy + fz + (fx, fy, fz)[c])
    return outs


def main_kernel(
    pos_ref, off_ref, den_ref, f_ref, bd_ref, bf_ref, xu_ref, xd_ref, ext_ref, g_ref, coef_ref, mom_ref,
    dext_ref, s_ref, rwt_ref, w_ref,
):
    gx, gy = pos_ref[0], pos_ref[1]
    load_weights(off_ref, w_ref)
    sub, lane = sub_iota(ROWS), lane_iota(ROWS)
    y = jnp.where(sub < 12, sub, sub - 16) + gy * CY

    def in_y(at):
        return ((at >= 0) & (at < NY)).astype(F32)

    iy = {dy: in_y(y + dy) for dy in (-1, 0, 1)}
    iz = {dz: ((lane + dz >= 0) & (lane + dz < CZ)).astype(F32) for dz in (-1, 0, 1)}

    for case, dxs in enumerate(((0, 1), (-1, 0, 1), (-1, 0))):
        total = jnp.zeros((ROWS, CZ), F32)
        for dy in (-1, 0, 1):
            part = jnp.zeros((ROWS, CZ), F32)
            for dz in (-1, 0, 1):
                w = w_ref[(dxs[0] + 1) * 9 + (dy + 1) * 3 + dz + 1]
                for dx in dxs[1:]:
                    w = w + w_ref[(dx + 1) * 9 + (dy + 1) * 3 + dz + 1]
                part = part + w * iz[dz]
            total = total + part * iy[dy]
        rwt_ref[case] = jnp.where(total > 0.0, iy[0] / jnp.where(total > 0.0, total, 1.0), 0.0)

    for j in range(4):
        dext_ref[j] = xd_ref[j]
        dext_ref[20 + j] = xu_ref[j]
    for c in range(3):
        for j in range(3):
            ext_ref[c, j] = xd_ref[4 + 3 * c + j]
            ext_ref[c, 19 + j] = xu_ref[4 + 3 * c + j]

    def spread(x, _):
        dext_ref[x + 4, 0:8] = den_ref[x]
        dext_ref[x + 4, 8:16] = bd_ref[x]
        for c in range(3):
            ext_ref[c, x + 3, 0:8] = f_ref[c, x]
            ext_ref[c, x + 3, 8:16] = bf_ref[c, x]
        return 0

    lax.fori_loop(0, CX, spread, 0, unroll=2)

    low_half = (sub_iota(8) < 4)

    def smooth_step(p, _):
        x = gx * CX + p - 3
        planes = [dext_ref[p], dext_ref[p + 1], dext_ref[p + 2]]
        num = filter_plane(planes, w_ref, lane, 1)
        case = jnp.where(x == 0, 0, jnp.where(x == NX - 1, 2, 1))
        in_x = jnp.where((x >= 0) & (x < NX), jnp.float32(1.0), jnp.float32(0.0))
        rwt = rwt_ref[case] * in_x
        smooth = num * rwt
        mask = jnp.concatenate(
            [
                jnp.where(low_half, ext_ref[1, p, 11:12], ext_ref[1, p, 12:13]),
                jnp.where(low_half, ext_ref[0, p, 11:12], ext_ref[0, p, 12:13]),
            ],
            axis=0,
        )
        sq = mask * (smooth * smooth)
        s_ref[p] = (iy[0] * in_x) * (EMIN + (sq * smooth) * (1.0 - EMIN))
        coef_ref[p] = (-3.0 * (1.0 - EMIN)) * sq * rwt
        return 0

    lax.fori_loop(0, CX + 6, smooth_step, 0)

    def image_step(q, _):
        x = gx * CX + q - 2
        in_x = jnp.where((x >= 0) & (x < NX), jnp.float32(1.0), jnp.float32(0.0))
        inside = iy[0] * in_x
        outs = image_plane(
            lambda c, k: ext_ref[c, q + 1 + k], s_ref[q], s_ref[q + 1], s_ref[q + 2], lane
        )
        for c in range(3):
            g_ref[c, q] = outs[c] * inside
        return 0

    lax.fori_loop(0, CX + 4, image_step, 0)

    def moment_step(x, sums):
        outs = image_plane(
            lambda c, k: g_ref[c, x + 2 + k], s_ref[x + 2], s_ref[x + 3], s_ref[x + 4], lane
        )
        m0, m1, m2, m3 = sums
        for c in range(3):
            f, g = f_ref[c, x], g_ref[c, x + 2, 0:8]
            m0, m1, m2, m3 = m0 + f * f, m1 + f * g, m2 + g * g, m3 + g * outs[c][0:8]
        return m0, m1, m2, m3

    zero = jnp.zeros((8, CZ), F32)
    sums = lax.fori_loop(0, CX, moment_step, (zero, zero, zero, zero))
    at = lax.broadcasted_iota(jnp.int32, (1, 128), 1)
    line = jnp.zeros((1, 128), F32)
    for k in range(4):
        total = jnp.sum(jnp.sum(sums[k], axis=0, keepdims=True), axis=1, keepdims=True)
        line = jnp.where(at == k, total, line)
    mom_ref[...] = line


def last_kernel(off_ref, ext_ref, g_ref, coef_ref, mom_ref, u_out, sens_out, u_ref, sh_ref, w_ref):
    load_weights(off_ref, w_ref)
    lane = lane_iota(ROWS)
    line = jnp.sum(mom_ref[...], axis=0, keepdims=True)
    at = lax.broadcasted_iota(jnp.int32, (1, 128), 1)
    m0, m1, m2, m3 = (
        jnp.sum(jnp.where(at == k, line, 0.0), axis=1, keepdims=True) for k in range(4)
    )
    s1 = m0 / m1
    rr = m0 - 2.0 * s1 * m1 + s1 * s1 * m2
    grow = 1.0 + rr / m0
    s2 = rr / (grow * grow * m1 - 2.0 * grow * s1 * m2 + s1 * s1 * m3)
    alpha = jnp.broadcast_to(s1 + s2 * grow, (ROWS, CZ))
    beta = jnp.broadcast_to(-s1 * s2, (ROWS, CZ))

    def u_step(q, _):
        for c in range(3):
            u_ref[c, q] = alpha * ext_ref[c, q + 1] + beta * g_ref[c, q]
        return 0

    lax.fori_loop(0, CX + 4, u_step, 0)

    def share_step(r, _):
        ex = ey = ez = e0 = None
        for c in range(3):
            v = u_ref[c, r + 1]
            ax, bx = v - u_ref[c, r + 2], v - u_ref[c, r]
            ay, az = v - yp(v), v - zp(v, lane)
            tx, ty, tz, t0 = ax * ax + bx * bx, ay * ay, az * az, v * v
            if c == 0:
                tx = tx + tx
            elif c == 1:
                ty = ty + ty
            else:
                tz, t0 = tz + tz, t0 + t0
            ex = tx if ex is None else ex + tx
            ey = ty if ey is None else ey + ty
            ez = tz if ez is None else ez + tz
            e0 = t0 if e0 is None else e0 + t0
        energy = 0.5 * (ex + (ey + ym(ey)) + (ez + zm(ez, lane, e0)))
        sh_ref[r] = coef_ref[r + 2] * energy
        return 0

    lax.fori_loop(0, CX + 2, share_step, 0)

    def out_step(x, _):
        planes = [sh_ref[x], sh_ref[x + 1], sh_ref[x + 2]]
        sens_out[x] = filter_plane(planes, w_ref, lane, -1)[0:8]
        for c in range(3):
            u_out[c, x] = u_ref[c, x + 2, 0:8]
        return 0

    lax.fori_loop(0, CX, out_step, 0)


VMEM = pl.BlockSpec(memory_space=pltpu.VMEM)
SMEM = pl.BlockSpec(memory_space=pltpu.SMEM)


def f32(*shape):
    return jax.ShapeDtypeStruct(shape, F32)


def call(kernel, outs, ins, scratch=()):
    return pl.pallas_call(
        kernel,
        out_shape=outs,
        in_specs=ins,
        out_specs=jax.tree.map(lambda _: VMEM, outs),
        scratch_shapes=list(scratch),
        compiler_params=pltpu.CompilerParams(vmem_limit_bytes=40 * 1024 * 1024),
    )


def swap(lo, hi, axes, count):
    up = lax.ppermute(lo, axes, [(i + 1, i) for i in range(count - 1)])
    down = lax.ppermute(hi, axes, [(i, i + 1) for i in range(count - 1)])
    return up, down


def spread_sum(line, axes, count):
    lines = jnp.broadcast_to(line, (count, 128))
    return lax.all_to_all(lines, axes, 0, 0, tiled=True)


def body(density, force, brick_ids, offsets):
    gx, gy = ("zl", "x"), ("zh", "y", "c")
    pos = jnp.stack([lax.axis_index(gx), lax.axis_index(gy)]).astype(jnp.int32)
    ids = brick_ids.reshape(1, 512)
    slab_y = f32(CX, ROWS, CZ)
    lo, hi, mask = call(pack_y_kernel, (slab_y, slab_y, f32(8, CZ)), [VMEM] * 3)(density, force, ids)
    up, down = swap(lo, hi, gy, 64)
    slab_x = f32(13, ROWS, CZ)
    bd, bf, lo, hi = call(
        pack_x_kernel, (f32(CX, 8, CZ), f32(3, CX, 8, CZ), slab_x, slab_x), [VMEM] * 5
    )(density, force, mask, up, down)
    up, down = swap(lo, hi, gx, 12)
    ext, image, coef, line = call(
        main_kernel,
        (f32(3, CX + 6, ROWS, CZ), f32(3, CX + 4, ROWS, CZ), f32(CX + 6, ROWS, CZ), f32(1, 128)),
        [SMEM, SMEM] + [VMEM] * 6,
        [
            pltpu.VMEM((CX + 8, ROWS, CZ), F32),
            pltpu.VMEM((CX + 6, ROWS, CZ), F32),
            pltpu.VMEM((3, ROWS, CZ), F32),
            pltpu.SMEM((27,), F32),
        ],
    )(pos, offsets, density, force, bd, bf, up, down)
    lines = spread_sum(line, ("x", "y"), 32)
    lines = spread_sum(jnp.sum(lines, axis=0, keepdims=True), ("zl", "zh", "c"), 24)
    return call(
        last_kernel,
        (f32(3, CX, CY, CZ), f32(CX, CY, CZ)),
        [SMEM] + [VMEM] * 4,
        [
            pltpu.VMEM((3, CX + 4, ROWS, CZ), F32),
            pltpu.VMEM((CX + 2, ROWS, CZ), F32),
            pltpu.SMEM((27,), F32),
        ],
    )(offsets, ext, image, coef, lines)


def solution(mesh):
    fine = Mesh(mesh.devices.reshape(3, 4, 4, 8, 2), ("zl", "x", "zh", "y", "c"))
    gx, gy = ("zl", "x"), ("zh", "y", "c")
    return jax.shard_map(
        body,
        mesh=fine,
        in_specs=(P(gx, gy, None), P(None, gx, gy, None), P(gx, gy, None), P()),
        out_specs=(P(None, gx, gy, None), P(gx, gy, None)),
        check_vma=False,
    )
```

```python
import functools

import jax
import jax.numpy as jnp
import numpy as np
from jax import lax
from jax.experimental import pallas as pl
from jax.experimental.pallas import tpu as pltpu
from jax.sharding import Mesh
from jax.sharding import PartitionSpec as P

EMIN = 0.001
RADIUS = 2.0
REACH = [float(np.float32(RADIUS) - np.float32(np.sqrt(np.float32(s)))) for s in range(4)]

CX, CY, CZ = 16, 8, 256
NX, NY = 192, 512
DEV_X, DEV_Y = 12, 64
ROWS = 16
F32 = jnp.float32
UNROLL = (11, 4, 4, 6, 4)


def sub_iota(rows):
    return lax.broadcasted_iota(jnp.int32, (rows, CZ), 0)


def lane_iota(rows):
    return lax.broadcasted_iota(jnp.int32, (rows, CZ), 1)


def roll(v, shift, axis):
    return pltpu.roll(v, shift % v.shape[axis], axis)


def yp(v):
    return roll(v, -1, 0)


def ym(v):
    return roll(v, 1, 0)


def zp(v, lane, fill=0.0):
    return jnp.where(lane == CZ - 1, fill, roll(v, -1, 1))


def zm(v, lane, fill=0.0):
    return jnp.where(lane == 0, fill, roll(v, 1, 1))


def store_weights(off_ref, w_ref):
    for i in range(27):
        w_ref[i] = jnp.float32(0.0)
    for j in range(off_ref.shape[1]):
        dx, dy, dz = off_ref[0, j], off_ref[1, j], off_ref[2, j]
        s = dx * dx + dy * dy + dz * dz
        w = jnp.where(
            s == 0,
            jnp.float32(REACH[0]),
            jnp.where(
                s == 1,
                jnp.float32(REACH[1]),
                jnp.where(s == 2, jnp.float32(REACH[2]), jnp.float32(REACH[3])),
            ),
        )
        w_ref[(dx + 1) * 9 + (dy + 1) * 3 + dz + 1] = w


def pack_kernel(
    off_ref, den_hbm, f_hbm, ids_hbm,
    den_ref, f_ref, m_ref, w_ref, ylo_ref, yhi_ref, xlo_ref, xhi_ref, ll_ref, lh_ref, hl_ref, hh_ref,
    ids_ref, sem,
):
    copies = [
        pltpu.make_async_copy(src, dst, sem.at[i])
        for i, (src, dst) in enumerate(((ids_hbm, ids_ref), (den_hbm, den_ref), (f_hbm, f_ref)))
    ]
    for copy in copies:
        copy.start()
    store_weights(off_ref, w_ref)
    copies[0].wait()
    ids = ids_ref[...]
    row = lax.shift_right_logical(ids, 6)
    col = lax.bitwise_and(ids, 63)
    p = (lax.broadcasted_iota(jnp.int32, (8, 512), 0) == row).astype(jnp.bfloat16)
    q = (
        lax.shift_right_logical(lax.broadcasted_iota(jnp.int32, (CZ, 512), 0), 2) == col
    ).astype(jnp.bfloat16)
    m_ref[...] = lax.dot_general(p, q, (((1,), (1,)), ((), ())), preferred_element_type=F32)
    sub = sub_iota(8)
    low = sub < 4
    copies[1].wait()
    copies[2].wait()

    for x in range(CX):
        base = x // 4 * 2
        m_lo, m_hi = m_ref[base : base + 1], m_ref[base + 1 : base + 2]
        den, f0, f1, f2 = den_ref[x], f_ref[0, x], f_ref[1, x], f_ref[2, x]
        f0r, f2r = roll(f0, 4, 0), roll(f2, 4, 0)
        lo0 = jnp.where(sub == 7, m_lo, jnp.where(low, den, f0r))
        lo1 = jnp.where(low, f1, f2r)
        hi0 = jnp.where(sub == 0, m_hi, jnp.where(low, f0r, den))
        hi1 = jnp.where(low, f2r, f1)
        for ref, t0, t1 in ((ylo_ref, lo0, lo1), (yhi_ref, hi0, hi1)):
            ref[x, 0:8] = t0
            ref[x, 8:16] = t1
        if x < 4 or x >= 12:
            for ref, t0, t1 in (
                ((ll_ref, lo0, lo1), (lh_ref, hi0, hi1))
                if x < 4
                else ((hl_ref, lo0, lo1), (hh_ref, hi0, hi1))
            ):
                ref[x % 4, 0:8] = t0
                ref[x % 4, 8:16] = t1
            slab = xlo_ref if x < 4 else xhi_ref
            slab[x % 4] = den
            at = x if x < 4 else x - 13
            if 0 <= at < 3:
                for c, f in enumerate((f0, f1, f2)):
                    slab[4 + 3 * c + at] = f
            if x == 0 or x == 12:
                slab[13] = jnp.where(low, m_lo, m_hi)


def filter_plane(planes, w_ref, lane, sign):
    out = None
    for dz in (-1, 0, 1):
        acc = None
        for dy in (-1, 0, 1):
            t = None
            for dx in (-1, 0, 1):
                w = w_ref[(sign * dx + 1) * 9 + (sign * dy + 1) * 3 + sign * dz + 1]
                term = planes[dx + 1] * w
                t = term if t is None else t + term
            if dy == 1:
                t = yp(t)
            elif dy == -1:
                t = ym(t)
            acc = t if acc is None else acc + t
        if dz == 1:
            acc = zp(acc, lane)
        elif dz == -1:
            acc = zm(acc, lane)
        out = acc if out is None else out + acc
    return out


def image_plane(load, s_m, s_0, s_p, lane):
    px, mx = 0.5 * (s_0 + s_p), 0.5 * (s_0 + s_m)
    py = 0.5 * (s_0 + yp(s_0))
    pz = 0.5 * (s_0 + zp(s_0, lane))
    half = -0.5 * s_0
    outs = []
    for c in range(3):
        v = load(c, 0)
        fx = px * (v - load(c, 1)) + mx * (v - load(c, -1))
        fy = py * (v - yp(v))
        fy = fy - ym(fy)
        fz = pz * (v - zp(v, lane))
        fz = fz - zm(fz, lane, half * v)
        outs.append(fx + fy + fz + (fx, fy, fz)[c])
    return outs


def main_kernel(
    pos_ref, w_ref, den_ref, f_ref, m_ref, yu_ref, yd_ref, xu_ref, xd_ref, uu_ref, ud_ref, du_ref, dd_ref,
    ext_ref, g_ref, coef_ref, mom_ref,
    dext_ref, s_ref, rwt_ref, mask_ref,
):
    gx, gy = pos_ref[0], pos_ref[1]
    sub, lane = sub_iota(ROWS), lane_iota(ROWS)
    y = jnp.where(sub < 12, sub, sub - 16) + gy * CY

    def in_y(at):
        return ((at >= 0) & (at < NY)).astype(F32)

    iy = {dy: in_y(y + dy) for dy in (-1, 0, 1)}
    iz = {dz: ((lane + dz >= 0) & (lane + dz < CZ)).astype(F32) for dz in (-1, 0, 1)}

    for case, dxs in enumerate(((0, 1), (-1, 0, 1), (-1, 0))):
        total = jnp.zeros((ROWS, CZ), F32)
        for dy in (-1, 0, 1):
            part = jnp.zeros((ROWS, CZ), F32)
            for dz in (-1, 0, 1):
                w = w_ref[(dxs[0] + 1) * 9 + (dy + 1) * 3 + dz + 1]
                for dx in dxs[1:]:
                    w = w + w_ref[(dx + 1) * 9 + (dy + 1) * 3 + dz + 1]
                part = part + w * iz[dz]
            total = total + part * iy[dy]
        rwt_ref[case] = jnp.where(total > 0.0, iy[0] / jnp.where(total > 0.0, total, 1.0), 0.0)

    sub8 = sub_iota(8)
    low = sub8 < 4
    for layer in range(6):
        if layer == 0:
            own, up, down = xd_ref[13], du_ref[0, 7:8], dd_ref[0, 0:1]
        elif layer == 5:
            own, up, down = xu_ref[13], uu_ref[0, 7:8], ud_ref[0, 0:1]
        else:
            k, x = 2 * (layer - 1), 4 * (layer - 1)
            own = jnp.where(low, m_ref[k : k + 1], m_ref[k + 1 : k + 2])
            up, down = yu_ref[x, 7:8], yd_ref[x, 0:1]
        mask_ref[layer, 0:8] = own
        mask_ref[layer, 8:16] = jnp.where(low, up, down)

    def spread(j, den, fs, u0, u1, d0, d1):
        dext_ref[j, 0:8] = den
        dext_ref[j, 8:16] = jnp.where(low, u0, d0)
        if fs is None:
            return
        halo = (
            roll(jnp.where(low, d0, u0), 4, 0),
            jnp.where(low, u1, d1),
            roll(jnp.where(low, d1, u1), 4, 0),
        )
        for c in range(3):
            ext_ref[c, j - 1, 0:8] = fs[c]
            ext_ref[c, j - 1, 8:16] = halo[c]

    for i in range(4):
        for at, first, side, up, down in ((i, 1, xd_ref, du_ref, dd_ref), (20 + i, 0, xu_ref, uu_ref, ud_ref)):
            k = i - first
            fs = [side[4 + 3 * c + k] for c in range(3)] if 0 <= k < 3 else None
            spread(at, side[i], fs, up[i, 0:8], up[i, 8:16], down[i, 0:8], down[i, 8:16])

    def spread_own(x, _):
        fs = [f_ref[c, x] for c in range(3)]
        spread(x + 4, den_ref[x], fs, yu_ref[x, 0:8], yu_ref[x, 8:16], yd_ref[x, 0:8], yd_ref[x, 8:16])
        return 0

    lax.fori_loop(0, CX, spread_own, 0, unroll=4)

    def smooth_step(p, _):
        x = gx * CX + p - 3
        planes = [dext_ref[p], dext_ref[p + 1], dext_ref[p + 2]]
        num = filter_plane(planes, w_ref, lane, 1)
        case = jnp.where(x == 0, 0, jnp.where(x == NX - 1, 2, 1))
        in_x = jnp.where((x >= 0) & (x < NX), jnp.float32(1.0), jnp.float32(0.0))
        rwt = rwt_ref[case] * in_x
        smooth = num * rwt
        mask = mask_ref[lax.shift_right_logical(p + 1, 2)]
        sq = mask * (smooth * smooth)
        s_ref[p] = (iy[0] * in_x) * (EMIN + (sq * smooth) * (1.0 - EMIN))
        coef_ref[p] = (-3.0 * (1.0 - EMIN)) * sq * rwt
        return 0

    lax.fori_loop(0, CX + 6, smooth_step, 0, unroll=UNROLL[0])

    def image_step(q, _):
        x = gx * CX + q - 2
        in_x = jnp.where((x >= 0) & (x < NX), jnp.float32(1.0), jnp.float32(0.0))
        inside = iy[0] * in_x
        outs = image_plane(
            lambda c, k: ext_ref[c, q + 1 + k], s_ref[q], s_ref[q + 1], s_ref[q + 2], lane
        )
        for c in range(3):
            g_ref[c, q] = outs[c] * inside
        return 0

    lax.fori_loop(0, CX + 4, image_step, 0, unroll=UNROLL[1])

    def moment_step(x, sums):
        outs = image_plane(
            lambda c, k: g_ref[c, x + 2 + k], s_ref[x + 2], s_ref[x + 3], s_ref[x + 4], lane
        )
        m0, m1, m2, m3 = sums
        for c in range(3):
            f, g = f_ref[c, x], g_ref[c, x + 2, 0:8]
            m0, m1, m2, m3 = m0 + f * f, m1 + f * g, m2 + g * g, m3 + g * outs[c][0:8]
        return m0, m1, m2, m3

    zero = jnp.zeros((8, CZ), F32)
    sums = lax.fori_loop(0, CX, moment_step, (zero, zero, zero, zero), unroll=UNROLL[2])
    at = lax.broadcasted_iota(jnp.int32, (1, 128), 1)
    line = jnp.zeros((1, 128), F32)
    for k in range(4):
        total = jnp.sum(jnp.sum(sums[k], axis=0, keepdims=True), axis=1, keepdims=True)
        line = jnp.where(at == k, total, line)
    mom_ref[...] = line


def last_kernel(
    w_ref, ext_ref, g_ref, coef_ref, mom_ref, u_hbm, sens_hbm, u_ref, sh_ref, own_ref, sens_ref, sem
):
    lane = lane_iota(ROWS)
    line = jnp.sum(mom_ref[...], axis=0, keepdims=True)
    at = lax.broadcasted_iota(jnp.int32, (1, 128), 1)
    m0, m1, m2, m3 = (
        jnp.sum(jnp.where(at == k, line, 0.0), axis=1, keepdims=True) for k in range(4)
    )
    s1 = m0 / m1
    rr = m0 - 2.0 * s1 * m1 + s1 * s1 * m2
    grow = 1.0 + rr / m0
    s2 = rr / (grow * grow * m1 - 2.0 * grow * s1 * m2 + s1 * s1 * m3)
    alpha = jnp.broadcast_to(s1 + s2 * grow, (ROWS, CZ))
    beta = jnp.broadcast_to(-s1 * s2, (ROWS, CZ))

    def u_plane(q):
        us = [alpha * ext_ref[c, q + 1] + beta * g_ref[c, q] for c in range(3)]
        for c in range(3):
            u_ref[c, q] = us[c]
        return us

    def u_step(x, _):
        us = u_plane(x + 2)
        for c in range(3):
            own_ref[c, x] = us[c][0:8]
        return 0

    lax.fori_loop(0, CX, u_step, 0, unroll=4)
    u_copy = pltpu.make_async_copy(own_ref, u_hbm, sem.at[0])
    u_copy.start()
    for q in (0, 1, CX + 2, CX + 3):
        u_plane(q)

    def share_step(r, _):
        ex = ey = ez = e0 = None
        for c in range(3):
            v = u_ref[c, r + 1]
            ax, bx = v - u_ref[c, r + 2], v - u_ref[c, r]
            ay, az = v - yp(v), v - zp(v, lane)
            tx, ty, tz, t0 = ax * ax + bx * bx, ay * ay, az * az, v * v
            if c == 0:
                tx = tx + tx
            elif c == 1:
                ty = ty + ty
            else:
                tz, t0 = tz + tz, t0 + t0
            ex = tx if ex is None else ex + tx
            ey = ty if ey is None else ey + ty
            ez = tz if ez is None else ez + tz
            e0 = t0 if e0 is None else e0 + t0
        energy = 0.5 * (ex + (ey + ym(ey)) + (ez + zm(ez, lane, e0)))
        sh_ref[r] = coef_ref[r + 2] * energy
        return 0

    lax.fori_loop(0, CX + 2, share_step, 0, unroll=UNROLL[3])

    def out_step(x, _):
        planes = [sh_ref[x], sh_ref[x + 1], sh_ref[x + 2]]
        sens_ref[x] = filter_plane(planes, w_ref, lane, -1)[0:8]
        return 0

    half = CX // 2
    copies = [u_copy]
    for k in range(2):
        lax.fori_loop(k * half, (k + 1) * half, out_step, 0, unroll=UNROLL[4])
        part = pl.ds(k * half, half)
        copies.append(pltpu.make_async_copy(sens_ref.at[part], sens_hbm.at[part], sem.at[1 + k]))
        copies[-1].start()
    for copy in copies:
        copy.wait()


VMEM = pl.BlockSpec(memory_space=pltpu.VMEM)
SMEM = pl.BlockSpec(memory_space=pltpu.SMEM)


def f32(*shape):
    return jax.ShapeDtypeStruct(shape, F32)


HBM = pl.BlockSpec(memory_space=pltpu.HBM)


def call(kernel, outs, ins, out_specs, scratch):
    return pl.pallas_call(
        kernel,
        out_shape=outs,
        in_specs=ins,
        out_specs=out_specs,
        scratch_shapes=scratch,
        compiler_params=pltpu.CompilerParams(vmem_limit_bytes=24 * 1024 * 1024),
    )


def shift(slab, dx, dy):
    pairs = [
        (i * DEV_Y + j, (i + dx) * DEV_Y + j + dy)
        for i in range(DEV_X)
        for j in range(DEV_Y)
        if 0 <= i + dx < DEV_X and 0 <= j + dy < DEV_Y
    ]
    return lax.ppermute(slab, ("zl", "x", "zh", "y", "c"), pairs)


def spread_sum(line, axes, count):
    lines = jnp.broadcast_to(line, (count, 128))
    return lax.all_to_all(lines, axes, 0, 0, tiled=True)


def body(density, force, brick_ids, offsets):
    gx, gy = ("zl", "x"), ("zh", "y", "c")
    pos = jnp.stack([lax.axis_index(gx), lax.axis_index(gy)]).astype(jnp.int32)
    ids = brick_ids.reshape(1, 512)
    slab_y, slab_x, corner = f32(CX, ROWS, CZ), f32(14, 8, CZ), f32(4, ROWS, CZ)
    den, f, mask, w, ylo, yhi, xlo, xhi, ll, lh, hl, hh = call(
        pack_kernel,
        (f32(CX, CY, CZ), f32(3, CX, CY, CZ), f32(8, CZ), f32(27), slab_y, slab_y, slab_x, slab_x)
        + (corner,) * 4,
        [SMEM, HBM, HBM, HBM],
        (VMEM, VMEM, VMEM, SMEM) + (VMEM,) * 8,
        [pltpu.VMEM((1, 512), jnp.int32), pltpu.SemaphoreType.DMA((3,))],
    )(*(pltpu.with_memory_space_constraint(a, pltpu.HBM) for a in (offsets.T, density, force, ids)))
    yu, yd = shift(ylo, 0, -1), shift(yhi, 0, 1)
    xu, xd = shift(xlo, -1, 0), shift(xhi, 1, 0)
    uu, ud, du, dd = shift(ll, -1, -1), shift(lh, -1, 1), shift(hl, 1, -1), shift(hh, 1, 1)
    ext, image, coef, line = call(
        main_kernel,
        (f32(3, CX + 6, ROWS, CZ), f32(3, CX + 4, ROWS, CZ), f32(CX + 6, ROWS, CZ), f32(1, 128)),
        [SMEM, SMEM] + [VMEM] * 11,
        (VMEM,) * 4,
        [
            pltpu.VMEM((CX + 8, ROWS, CZ), F32),
            pltpu.VMEM((CX + 6, ROWS, CZ), F32),
            pltpu.VMEM((3, ROWS, CZ), F32),
            pltpu.VMEM((6, ROWS, CZ), F32),
        ],
    )(pos, w, den, f, mask, yu, yd, xu, xd, uu, ud, du, dd)
    lines = spread_sum(line, ("x", "y"), 32)
    lines = spread_sum(jnp.sum(lines, axis=0, keepdims=True), ("zl", "zh", "c"), 24)
    return call(
        last_kernel,
        (f32(3, CX, CY, CZ), f32(CX, CY, CZ)),
        [SMEM] + [VMEM] * 4,
        (HBM, HBM),
        [
            pltpu.VMEM((3, CX + 4, ROWS, CZ), F32),
            pltpu.VMEM((CX + 2, ROWS, CZ), F32),
            pltpu.VMEM((3, CX, CY, CZ), F32),
            pltpu.VMEM((CX, CY, CZ), F32),
            pltpu.SemaphoreType.DMA((3,)),
        ],
    )(w, ext, image, coef, lines)


def solution(mesh):
    fine = Mesh(mesh.devices.reshape(3, 4, 4, 8, 2), ("zl", "x", "zh", "y", "c"))
    gx, gy = ("zl", "x"), ("zh", "y", "c")
    return jax.shard_map(
        body,
        mesh=fine,
        in_specs=(P(gx, gy, None), P(None, gx, gy, None), P(gx, gy, None), P()),
        out_specs=(P(None, gx, gy, None), P(gx, gy, None)),
        check_vma=False,
    )
```

```python
import functools

import jax
import jax.numpy as jnp
import numpy as np
from jax import lax
from jax.experimental import pallas as pl
from jax.experimental.pallas import tpu as pltpu
from jax.sharding import Mesh
from jax.sharding import PartitionSpec as P

EMIN = 0.001
RADIUS = 2.0
REACH = [float(np.float32(RADIUS) - np.float32(np.sqrt(np.float32(s)))) for s in range(4)]

CX, CY, CZ = 16, 8, 256
NX, NY = 192, 512
DEV_X, DEV_Y = 12, 64
ROWS = 16
F32 = jnp.float32
UNROLL = (7, 4, 5, 8, 4, 1, 6, 4)


def sub_iota(rows):
    return lax.broadcasted_iota(jnp.int32, (rows, CZ), 0)


def lane_iota(rows):
    return lax.broadcasted_iota(jnp.int32, (rows, CZ), 1)


def roll(v, shift, axis):
    return pltpu.roll(v, shift % v.shape[axis], axis)


def yp(v):
    return roll(v, -1, 0)


def ym(v):
    return roll(v, 1, 0)


def zp(v, lane, fill=0.0):
    return jnp.where(lane == CZ - 1, fill, roll(v, -1, 1))


def zm(v, lane, fill=0.0):
    return jnp.where(lane == 0, fill, roll(v, 1, 1))


def store_weights(off_ref, w_ref):
    for i in range(27):
        w_ref[i] = jnp.float32(0.0)
    for j in range(off_ref.shape[1]):
        dx, dy, dz = off_ref[0, j], off_ref[1, j], off_ref[2, j]
        s = dx * dx + dy * dy + dz * dz
        w = jnp.where(
            s == 0,
            jnp.float32(REACH[0]),
            jnp.where(
                s == 1,
                jnp.float32(REACH[1]),
                jnp.where(s == 2, jnp.float32(REACH[2]), jnp.float32(REACH[3])),
            ),
        )
        w_ref[(dx + 1) * 9 + (dy + 1) * 3 + dz + 1] = w


def pack_y_kernel(
    off_ref, den_hbm, f_hbm, ids_hbm, den_ref, f_ref, m_ref, w_ref, lo_ref, hi_ref, ids_ref, sem
):
    copies = [
        pltpu.make_async_copy(src, dst, sem.at[i])
        for i, (src, dst) in enumerate(((ids_hbm, ids_ref), (den_hbm, den_ref), (f_hbm, f_ref)))
    ]
    for copy in copies:
        copy.start()
    store_weights(off_ref, w_ref)
    copies[0].wait()
    ids = ids_ref[...]
    row = lax.shift_right_logical(ids, 6)
    col = lax.bitwise_and(ids, 63)
    p = (lax.broadcasted_iota(jnp.int32, (8, 512), 0) == row).astype(jnp.bfloat16)
    q = (
        lax.shift_right_logical(lax.broadcasted_iota(jnp.int32, (CZ, 512), 0), 2) == col
    ).astype(jnp.bfloat16)
    flags = lax.dot_general(p, q, (((1,), (1,)), ((), ())), preferred_element_type=F32)
    m_ref[...] = flags
    lo_ref[208:216] = flags
    hi_ref[208:216] = flags
    copies[1].wait()
    den = jnp.swapaxes(den_ref[...], 0, 1)
    for j in range(4):
        lo_ref[16 * j : 16 * j + 16] = den[j]
        hi_ref[16 * j : 16 * j + 16] = den[4 + j]
    copies[2].wait()
    for c in range(3):
        f = jnp.swapaxes(f_ref[c], 0, 1)
        for j in range(3):
            at = 64 + 16 * (3 * c + j)
            lo_ref[at : at + 16] = f[j]
            hi_ref[at : at + 16] = f[5 + j]


def pack_x_kernel(den_ref, f_ref, m_ref, up_ref, dn_ref, dext_ref, fext_ref, lo_ref, hi_ref):
    def spread_flags(ref, first, by):
        rows = [ref[first + 2 * bx + by : first + 2 * bx + by + 1] for bx in range(4)]
        return jnp.concatenate([jnp.broadcast_to(r, (4, CZ)) for r in rows], axis=0)

    def halo_rows(planes):
        return jnp.swapaxes(jnp.stack(planes), 0, 1)

    dext_ref[:, 0:8] = den_ref[...]
    dext_ref[:, 8:16] = halo_rows(
        [up_ref[16 * j : 16 * j + 16] for j in range(4)] + [dn_ref[16 * j : 16 * j + 16] for j in range(4)]
    )
    flags = (
        [spread_flags(up_ref, 208, 0), spread_flags(dn_ref, 208, 1)],
        [spread_flags(m_ref, 0, 0), spread_flags(m_ref, 0, 1)],
        [jnp.zeros((CX, CZ), F32)] * 2,
    )
    for c in range(3):
        at = [64 + 16 * (3 * c + j) for j in range(3)]
        fext_ref[c, :, 0:8] = f_ref[c]
        fext_ref[c, :, 8:16] = halo_rows(
            [up_ref[i : i + 16] for i in at] + flags[c] + [dn_ref[i : i + 16] for i in at]
        )
    for slab, dx0, fx0 in ((lo_ref, 0, 0), (hi_ref, 12, 13)):
        slab[0:4] = dext_ref[dx0 : dx0 + 4]
        for c in range(3):
            slab[4 + 3 * c : 7 + 3 * c] = fext_ref[c, fx0 : fx0 + 3]


def filter_plane(planes, w_ref, lane, sign):
    out = None
    for dz in (-1, 0, 1):
        acc = None
        for dy in (-1, 0, 1):
            t = None
            for dx in (-1, 0, 1):
                w = w_ref[(sign * dx + 1) * 9 + (sign * dy + 1) * 3 + sign * dz + 1]
                term = planes[dx + 1] * w
                t = term if t is None else t + term
            if dy == 1:
                t = yp(t)
            elif dy == -1:
                t = ym(t)
            acc = t if acc is None else acc + t
        if dz == 1:
            acc = zp(acc, lane)
        elif dz == -1:
            acc = zm(acc, lane)
        out = acc if out is None else out + acc
    return out


def image_plane(load, s_m, s_0, s_p, lane):
    px, mx = 0.5 * (s_0 + s_p), 0.5 * (s_0 + s_m)
    py = 0.5 * (s_0 + yp(s_0))
    pz = 0.5 * (s_0 + zp(s_0, lane))
    half = -0.5 * s_0
    outs = []
    for c in range(3):
        v = load(c, 0)
        fx = px * (v - load(c, 1)) + mx * (v - load(c, -1))
        fy = py * (v - yp(v))
        fy = fy - ym(fy)
        fz = pz * (v - zp(v, lane))
        fz = fz - zm(fz, lane, half * v)
        outs.append(fx + fy + fz + (fx, fy, fz)[c])
    return outs


def grid_y(gy):
    sub = sub_iota(ROWS)
    y = jnp.where(sub < 12, sub, sub - 16) + gy * CY
    return {dy: ((y + dy >= 0) & (y + dy < NY)).astype(F32) for dy in (-1, 0, 1)}


def store_reciprocals(rwt_ref, w_ref, iy):
    lane = lane_iota(ROWS)
    iz = {dz: ((lane + dz >= 0) & (lane + dz < CZ)).astype(F32) for dz in (-1, 0, 1)}
    for case, dxs in enumerate(((0, 1), (-1, 0, 1), (-1, 0))):
        total = jnp.zeros((ROWS, CZ), F32)
        for dy in (-1, 0, 1):
            part = jnp.zeros((ROWS, CZ), F32)
            for dz in (-1, 0, 1):
                w = w_ref[(dxs[0] + 1) * 9 + (dy + 1) * 3 + dz + 1]
                for dx in dxs[1:]:
                    w = w + w_ref[(dx + 1) * 9 + (dy + 1) * 3 + dz + 1]
                part = part + w * iz[dz]
            total = total + part * iy[dy]
        rwt_ref[case] = jnp.where(total > 0.0, iy[0] / jnp.where(total > 0.0, total, 1.0), 0.0)


def on_grid(x):
    return jnp.where((x >= 0) & (x < NX), jnp.float32(1.0), jnp.float32(0.0))


def brick_flags(f1_rows, f0_rows):
    low = sub_iota(8) < 4
    halves = [jnp.where(low, rows[0:1], rows[1:2]) for rows in (f1_rows, f0_rows)]
    return jnp.concatenate(halves, axis=0)


def stiffness_plane(planes, flags, x, inside_y, rwt_ref, w_ref, lane):
    num = filter_plane(planes, w_ref, lane, 1)
    inside = on_grid(x)
    rwt = rwt_ref[jnp.where(x == 0, 0, jnp.where(x == NX - 1, 2, 1))] * inside
    smooth = num * rwt
    sq = flags * (smooth * smooth)
    stiff = (inside_y * inside) * (EMIN + (sq * smooth) * (1.0 - EMIN))
    return stiff, (-3.0 * (1.0 - EMIN)) * sq * rwt


def add_moments(sums, fs, gs, outs):
    m0, m1, m2, m3 = sums
    for f, g, out in zip(fs, gs, outs):
        f, g, out = f[0:8], g[0:8], out[0:8]
        m0, m1, m2, m3 = m0 + f * f, m1 + f * g, m2 + g * g, m3 + g * out
    return m0, m1, m2, m3


def inner_kernel(
    pos_ref, w_ref, dext_ref, fext_ref, s_ref, coef_ref, g_ref, sums_ref, rwt_ref
):
    gx, gy = pos_ref[0], pos_ref[1]
    lane = lane_iota(ROWS)
    iy = grid_y(gy)
    store_reciprocals(rwt_ref, w_ref, iy)

    def smooth_step(p, _):
        x = p + 1
        planes = [dext_ref[p], dext_ref[p + 1], dext_ref[p + 2]]
        flags = brick_flags(fext_ref[1, x, 11:13], fext_ref[0, x, 11:13])
        s_ref[p], coef_ref[p] = stiffness_plane(
            planes, flags, gx * CX + x, iy[0], rwt_ref, w_ref, lane
        )
        return 0

    lax.fori_loop(0, CX - 2, smooth_step, 0, unroll=UNROLL[0])

    def image_step(q, _):
        outs = image_plane(
            lambda c, k: fext_ref[c, q + 2 + k], s_ref[q], s_ref[q + 1], s_ref[q + 2], lane
        )
        for c in range(3):
            g_ref[c, q] = outs[c] * iy[0]
        return 0

    lax.fori_loop(0, CX - 4, image_step, 0, unroll=UNROLL[1])

    def moment_step(t, sums):
        outs = image_plane(
            lambda c, k: g_ref[c, t + 1 + k], s_ref[t + 1], s_ref[t + 2], s_ref[t + 3], lane
        )
        fs = [fext_ref[c, t + 3] for c in range(3)]
        return add_moments(sums, fs, [g_ref[c, t + 1] for c in range(3)], outs)

    zero = jnp.zeros((8, CZ), F32)
    sums = lax.fori_loop(0, CX - 6, moment_step, (zero,) * 4, unroll=UNROLL[2])
    for k in range(4):
        sums_ref[k] = sums[k]


def rim_kernel(
    pos_ref, w_ref, dext_ref, fext_ref, xu_ref, xd_ref, s_in_ref, g_in_ref, sums_ref, rwt_ref,
    g_ref, coef_ref, mom_ref,
    d2_ref, f2_ref, s2_ref, g2_ref,
):
    gx, gy = pos_ref[0], pos_ref[1]
    lane = lane_iota(ROWS)
    iy = grid_y(gy)
    d2_ref[0, 0:4] = xd_ref[0:4]
    d2_ref[0, 4:6] = dext_ref[0:2]
    d2_ref[1, 0:2] = dext_ref[14:16]
    d2_ref[1, 2:6] = xu_ref[0:4]
    s2_ref[0, 4:7] = s_in_ref[0:3]
    s2_ref[1, 0:3] = s_in_ref[11:14]
    for c in range(3):
        f2_ref[c, 0, 0:3] = xd_ref[4 + 3 * c : 7 + 3 * c]
        f2_ref[c, 0, 3:6] = fext_ref[c, 0:3]
        f2_ref[c, 1, 0:3] = fext_ref[c, 13:16]
        f2_ref[c, 1, 3:6] = xu_ref[4 + 3 * c : 7 + 3 * c]
        g2_ref[c, 0, 4:6] = g_in_ref[c, 0:2]
        g2_ref[c, 1, 0:2] = g_in_ref[c, 10:12]

    def smooth_step(i, _):
        side, m = lax.shift_right_logical(i, 2), lax.bitwise_and(i, 3)
        planes = [d2_ref[side, m + k] for k in range(3)]
        flags = brick_flags(f2_ref[1, side, m + 2 * side, 11:13], f2_ref[0, side, m + 2 * side, 11:13])
        s2_ref[side, m + 3 * side], coef_ref[side, m] = stiffness_plane(
            planes, flags, gx * CX + m - 3 + 18 * side, iy[0], rwt_ref, w_ref, lane
        )
        return 0

    lax.fori_loop(0, 8, smooth_step, 0, unroll=UNROLL[3])

    def image_step(i, _):
        side, m = lax.shift_right_logical(i, 2), lax.bitwise_and(i, 3)
        n = m + side
        outs = image_plane(
            lambda c, k: f2_ref[c, side, m + 1 + k],
            s2_ref[side, n], s2_ref[side, n + 1], s2_ref[side, n + 2], lane,
        )
        inside = iy[0] * on_grid(gx * CX + m - 2 + 16 * side)
        for c in range(3):
            g = outs[c] * inside
            g_ref[c, side, m] = g
            g2_ref[c, side, m + 2 * side] = g
        return 0

    lax.fori_loop(0, 8, image_step, 0, unroll=UNROLL[4])

    def moment_step(m, sums):
        for side in range(2):
            q = m + 2 - side
            n = m + 3 - 2 * side
            outs = image_plane(
                lambda c, k: g2_ref[c, side, q + k],
                s2_ref[side, n - 1], s2_ref[side, n], s2_ref[side, n + 1], lane,
            )
            fs = [f2_ref[c, side, m + 3 - 3 * side] for c in range(3)]
            sums = add_moments(sums, fs, [g2_ref[c, side, q] for c in range(3)], outs)
        return sums

    sums = lax.fori_loop(0, 3, moment_step, tuple(sums_ref[k] for k in range(4)), unroll=UNROLL[5])
    at = lax.broadcasted_iota(jnp.int32, (1, 128), 1)
    line = jnp.zeros((1, 128), F32)
    for k in range(4):
        total = jnp.sum(jnp.sum(sums[k], axis=0, keepdims=True), axis=1, keepdims=True)
        line = jnp.where(at == k, total, line)
    mom_ref[...] = line


def last_kernel(
    w_ref, fext_ref, xu_ref, xd_ref, g_in_ref, g_rim_ref, coef_in_ref, coef_rim_ref, mom_ref,
    u_hbm, sens_hbm,
    u_ref, sh_ref, coef_ref, own_ref, sens_ref, sem,
):
    lane = lane_iota(ROWS)
    line = jnp.sum(mom_ref[...], axis=0, keepdims=True)
    at = lax.broadcasted_iota(jnp.int32, (1, 128), 1)
    m0, m1, m2, m3 = (
        jnp.sum(jnp.where(at == k, line, 0.0), axis=1, keepdims=True) for k in range(4)
    )
    s1 = m0 / m1
    rr = m0 - 2.0 * s1 * m1 + s1 * s1 * m2
    grow = 1.0 + rr / m0
    s2 = rr / (grow * grow * m1 - 2.0 * grow * s1 * m2 + s1 * s1 * m3)
    alpha = jnp.broadcast_to(s1 + s2 * grow, (ROWS, CZ))
    beta = jnp.broadcast_to(-s1 * s2, (ROWS, CZ))

    def u_plane(q, fs, gs):
        us = [alpha * f + beta * g for f, g in zip(fs, gs)]
        for c in range(3):
            u_ref[c, q] = us[c]
        return us

    def u_step(k, _):
        us = u_plane(k + 4, [fext_ref[c, k + 2] for c in range(3)], [g_in_ref[c, k] for c in range(3)])
        for c in range(3):
            own_ref[c, k + 2] = us[c][0:8]
        return 0

    lax.fori_loop(0, CX - 4, u_step, 0, unroll=4)
    for x in (0, 1, 14, 15):
        side, m = (0, x + 2) if x < 8 else (1, x - 14)
        us = u_plane(
            x + 2, [fext_ref[c, x] for c in range(3)], [g_rim_ref[c, side, m] for c in range(3)]
        )
        for c in range(3):
            own_ref[c, x] = us[c][0:8]
    u_copy = pltpu.make_async_copy(own_ref, u_hbm, sem.at[0])
    u_copy.start()
    for q, slab, i, side, m in ((0, xd_ref, 1, 0, 0), (1, xd_ref, 2, 0, 1), (18, xu_ref, 0, 1, 2), (19, xu_ref, 1, 1, 3)):
        u_plane(q, [slab[4 + 3 * c + i] for c in range(3)], [g_rim_ref[c, side, m] for c in range(3)])
    coef_ref[0:2] = coef_rim_ref[0, 2:4]
    coef_ref[2:16] = coef_in_ref[...]
    coef_ref[16:18] = coef_rim_ref[1, 0:2]

    def share_step(r, _):
        ex = ey = ez = e0 = None
        for c in range(3):
            v = u_ref[c, r + 1]
            ax, bx = v - u_ref[c, r + 2], v - u_ref[c, r]
            ay, az = v - yp(v), v - zp(v, lane)
            tx, ty, tz, t0 = ax * ax + bx * bx, ay * ay, az * az, v * v
            if c == 0:
                tx = tx + tx
            elif c == 1:
                ty = ty + ty
            else:
                tz, t0 = tz + tz, t0 + t0
            ex = tx if ex is None else ex + tx
            ey = ty if ey is None else ey + ty
            ez = tz if ez is None else ez + tz
            e0 = t0 if e0 is None else e0 + t0
        energy = 0.5 * (ex + (ey + ym(ey)) + (ez + zm(ez, lane, e0)))
        sh_ref[r] = coef_ref[r] * energy
        return 0

    lax.fori_loop(0, CX + 2, share_step, 0, unroll=UNROLL[6])

    def out_step(x, _):
        planes = [sh_ref[x], sh_ref[x + 1], sh_ref[x + 2]]
        sens_ref[x] = filter_plane(planes, w_ref, lane, -1)[0:8]
        return 0

    half = CX // 2
    copies = [u_copy]
    for k in range(2):
        lax.fori_loop(k * half, (k + 1) * half, out_step, 0, unroll=UNROLL[7])
        part = pl.ds(k * half, half)
        copies.append(pltpu.make_async_copy(sens_ref.at[part], sens_hbm.at[part], sem.at[1 + k]))
        copies[-1].start()
    for copy in copies:
        copy.wait()


VMEM = pl.BlockSpec(memory_space=pltpu.VMEM)
SMEM = pl.BlockSpec(memory_space=pltpu.SMEM)


def f32(*shape):
    return jax.ShapeDtypeStruct(shape, F32)


HBM = pl.BlockSpec(memory_space=pltpu.HBM)


def call(kernel, outs, ins, out_specs, scratch, cost=None):
    return pl.pallas_call(
        kernel,
        out_shape=outs,
        in_specs=ins,
        out_specs=out_specs,
        scratch_shapes=scratch,
        cost_estimate=cost,
        compiler_params=pltpu.CompilerParams(vmem_limit_bytes=24 * 1024 * 1024),
    )


def swap(lo, hi, axes, count):
    up = lax.ppermute(lo, axes, [(i + 1, i) for i in range(count - 1)])
    down = lax.ppermute(hi, axes, [(i, i + 1) for i in range(count - 1)])
    return up, down


def spread_sum(line, axes, count):
    lines = jnp.broadcast_to(line, (count, 128))
    return lax.all_to_all(lines, axes, 0, 0, tiled=True)


def body(density, force, brick_ids, offsets):
    gx, gy = ("zl", "x"), ("zh", "y", "c")
    pos = jnp.stack([lax.axis_index(gx), lax.axis_index(gy)]).astype(jnp.int32)
    ins = (offsets.T, density, force, brick_ids.reshape(1, 512))
    plane = (ROWS, CZ)
    slab_y, slab_x = f32(216, CZ), f32(13, *plane)
    den, f, mask, w, lo, hi = call(
        pack_y_kernel,
        (f32(CX, CY, CZ), f32(3, CX, CY, CZ), f32(8, CZ), f32(27), slab_y, slab_y),
        [SMEM, HBM, HBM, HBM],
        (VMEM, VMEM, VMEM, SMEM, VMEM, VMEM),
        [pltpu.VMEM((1, 512), jnp.int32), pltpu.SemaphoreType.DMA((3,))],
    )(*(pltpu.with_memory_space_constraint(a, pltpu.HBM) for a in ins))
    up, down = swap(lo, hi, gy, DEV_Y)
    dext, fext, lo, hi = call(
        pack_x_kernel,
        (f32(CX, *plane), f32(3, CX, *plane), slab_x, slab_x),
        [VMEM] * 5,
        (VMEM,) * 4,
        [],
    )(den, f, mask, up, down)
    up, down = swap(lo, hi, gx, DEV_X)
    stiff, coef, image, sums, rwt = call(
        inner_kernel,
        (f32(14, *plane), f32(14, *plane), f32(3, 12, *plane), f32(4, 8, CZ), f32(3, *plane)),
        [SMEM, SMEM, VMEM, VMEM],
        (VMEM,) * 5,
        [],
        pl.CostEstimate(flops=8_000_000, bytes_accessed=8_000_000, transcendentals=0),
    )(pos, w, dext, fext)
    image_rim, coef_rim, line = call(
        rim_kernel,
        (f32(3, 2, 4, *plane), f32(2, 4, *plane), f32(1, 128)),
        [SMEM, SMEM] + [VMEM] * 8,
        (VMEM,) * 3,
        [
            pltpu.VMEM((2, 6, *plane), F32),
            pltpu.VMEM((3, 2, 6, *plane), F32),
            pltpu.VMEM((2, 7, *plane), F32),
            pltpu.VMEM((3, 2, 6, *plane), F32),
        ],
    )(pos, w, dext, fext, up, down, stiff, image, sums, rwt)
    lines = spread_sum(line, ("x", "y"), 32)
    lines = spread_sum(jnp.sum(lines, axis=0, keepdims=True), ("zl", "zh", "c"), 24)
    return call(
        last_kernel,
        (f32(3, CX, CY, CZ), f32(CX, CY, CZ)),
        [SMEM] + [VMEM] * 8,
        (HBM, HBM),
        [
            pltpu.VMEM((3, CX + 4, *plane), F32),
            pltpu.VMEM((CX + 2, *plane), F32),
            pltpu.VMEM((CX + 2, *plane), F32),
            pltpu.VMEM((3, CX, CY, CZ), F32),
            pltpu.VMEM((CX, CY, CZ), F32),
            pltpu.SemaphoreType.DMA((3,)),
        ],
    )(w, fext, up, down, image, image_rim, coef, coef_rim, lines)


def solution(mesh):
    fine = Mesh(mesh.devices.reshape(3, 4, 4, 8, 2), ("zl", "x", "zh", "y", "c"))
    gx, gy = ("zl", "x"), ("zh", "y", "c")
    return jax.shard_map(
        body,
        mesh=fine,
        in_specs=(P(gx, gy, None), P(None, gx, gy, None), P(gx, gy, None), P()),
        out_specs=(P(None, gx, gy, None), P(gx, gy, None)),
        check_vma=False,
    )
```

```python
import functools

import jax
import jax.numpy as jnp
import numpy as np
from jax import lax
from jax.experimental import pallas as pl
from jax.experimental.pallas import tpu as pltpu
from jax.sharding import Mesh
from jax.sharding import PartitionSpec as P

EMIN = 0.001
RADIUS = 2.0
REACH = [float(np.float32(RADIUS) - np.float32(np.sqrt(np.float32(s)))) for s in range(4)]

CX, CY, CZ = 16, 8, 256
NX, NY = 192, 512
DEV_X, DEV_Y = 12, 64
GX, GY = ("zl", "x"), ("zh", "y", "c")
ROWS = 16
F32 = jnp.float32
UNROLL = (7, 4, 5, 8, 4, 1, 6, 4)


def sub_iota(rows):
    return lax.broadcasted_iota(jnp.int32, (rows, CZ), 0)


def lane_iota(rows):
    return lax.broadcasted_iota(jnp.int32, (rows, CZ), 1)


def roll(v, shift, axis):
    return pltpu.roll(v, shift % v.shape[axis], axis)


def yp(v):
    return roll(v, -1, 0)


def ym(v):
    return roll(v, 1, 0)


def zp(v, lane, fill=0.0):
    return jnp.where(lane == CZ - 1, fill, roll(v, -1, 1))


def zm(v, lane, fill=0.0):
    return jnp.where(lane == 0, fill, roll(v, 1, 1))


def is_odd(at):
    return lax.bitwise_and(at, 1)


def store_weights(off_ref, w_ref):
    for i in range(27):
        w_ref[i] = jnp.float32(0.0)
    for j in range(off_ref.shape[1]):
        dx, dy, dz = off_ref[0, j], off_ref[1, j], off_ref[2, j]
        s = dx * dx + dy * dy + dz * dz
        w = jnp.where(
            s == 0,
            jnp.float32(REACH[0]),
            jnp.where(
                s == 1,
                jnp.float32(REACH[1]),
                jnp.where(s == 2, jnp.float32(REACH[2]), jnp.float32(REACH[3])),
            ),
        )
        w_ref[(dx + 1) * 9 + (dy + 1) * 3 + dz + 1] = w


def pack_y_kernel(
    den_hbm, f_hbm, ids_hbm, den_ref, f_ref, m_ref, first_ref, second_ref, ids_ref, sem
):
    copies = [
        pltpu.make_async_copy(src, dst, sem.at[i])
        for i, (src, dst) in enumerate(((ids_hbm, ids_ref), (den_hbm, den_ref), (f_hbm, f_ref)))
    ]
    for copy in copies:
        copy.start()
    copies[0].wait()
    ids = ids_ref[...]
    row = lax.shift_right_logical(ids, 6)
    col = lax.bitwise_and(ids, 63)
    p = (lax.broadcasted_iota(jnp.int32, (8, 512), 0) == row).astype(jnp.bfloat16)
    q = (
        lax.shift_right_logical(lax.broadcasted_iota(jnp.int32, (CZ, 512), 0), 2) == col
    ).astype(jnp.bfloat16)
    flags = lax.dot_general(p, q, (((1,), (1,)), ((), ())), preferred_element_type=F32)
    m_ref[...] = flags
    copies[1].wait()
    copies[2].wait()
    den = jnp.swapaxes(den_ref[...], 0, 1)
    fs = [jnp.swapaxes(f_ref[c], 0, 1) for c in range(3)]

    odd = jnp.full((CX, CZ), is_odd(lax.axis_index(GY)), jnp.int32) == 1

    def fill(at, lo, hi):
        first_ref[at : at + 16] = jnp.where(odd, hi, lo)
        second_ref[at : at + 16] = jnp.where(odd, lo, hi)

    first_ref[208:216] = flags
    second_ref[208:216] = flags
    for j in range(4):
        fill(16 * j, den[j], den[4 + j])
    for c in range(3):
        for j in range(3):
            fill(64 + 16 * (3 * c + j), fs[c][j], fs[c][5 + j])


def pack_x_kernel(
    den_ref, f_ref, m_ref, first_in, second_in, dext_ref, fext_ref, first_ref, second_ref
):
    odd_y = jnp.full((CX, CZ), is_odd(lax.axis_index(GY)), jnp.int32) == 1

    def below(first, count):
        return jnp.where(odd_y[0:count], second_in[first : first + count], first_in[first : first + count])

    def above(first, count):
        return jnp.where(odd_y[0:count], first_in[first : first + count], second_in[first : first + count])

    def spread_flags(flags, by):
        rows = [flags[2 * bx + by : 2 * bx + by + 1] for bx in range(4)]
        return jnp.concatenate([jnp.broadcast_to(r, (4, CZ)) for r in rows], axis=0)

    def halo_rows(planes):
        return jnp.swapaxes(jnp.stack(planes), 0, 1)

    dext_ref[:, 0:8] = den_ref[...]
    dext_ref[:, 8:16] = halo_rows(
        [above(16 * j, 16) for j in range(4)] + [below(16 * j, 16) for j in range(4)]
    )
    own = m_ref[...]
    flags = (
        [spread_flags(above(208, 8), 0), spread_flags(below(208, 8), 1)],
        [spread_flags(own, 0), spread_flags(own, 1)],
        [jnp.zeros((CX, CZ), F32)] * 2,
    )
    for c in range(3):
        at = [64 + 16 * (3 * c + j) for j in range(3)]
        fext_ref[c, :, 0:8] = f_ref[c]
        fext_ref[c, :, 8:16] = halo_rows(
            [above(i, 16) for i in at] + flags[c] + [below(i, 16) for i in at]
        )
    odd_x = is_odd(lax.axis_index(GX))
    for slab, top in ((first_ref, odd_x), (second_ref, 1 - odd_x)):
        slab[0:4] = dext_ref[pl.ds(12 * top, 4)]
        for c in range(3):
            slab[4 + 3 * c : 7 + 3 * c] = fext_ref[c, pl.ds(13 * top, 3)]


def filter_plane(planes, w_ref, lane, sign):
    out = None
    for dz in (-1, 0, 1):
        acc = None
        for dy in (-1, 0, 1):
            t = None
            for dx in (-1, 0, 1):
                w = w_ref[(sign * dx + 1) * 9 + (sign * dy + 1) * 3 + sign * dz + 1]
                term = planes[dx + 1] * w
                t = term if t is None else t + term
            if dy == 1:
                t = yp(t)
            elif dy == -1:
                t = ym(t)
            acc = t if acc is None else acc + t
        if dz == 1:
            acc = zp(acc, lane)
        elif dz == -1:
            acc = zm(acc, lane)
        out = acc if out is None else out + acc
    return out


def image_plane(load, s_m, s_0, s_p, lane):
    px, mx = 0.5 * (s_0 + s_p), 0.5 * (s_0 + s_m)
    py = 0.5 * (s_0 + yp(s_0))
    pz = 0.5 * (s_0 + zp(s_0, lane))
    half = -0.5 * s_0
    outs = []
    for c in range(3):
        v = load(c, 0)
        fx = px * (v - load(c, 1)) + mx * (v - load(c, -1))
        fy = py * (v - yp(v))
        fy = fy - ym(fy)
        fz = pz * (v - zp(v, lane))
        fz = fz - zm(fz, lane, half * v)
        outs.append(fx + fy + fz + (fx, fy, fz)[c])
    return outs


def grid_y(gy):
    sub = sub_iota(ROWS)
    y = jnp.where(sub < 12, sub, sub - 16) + gy * CY
    return {dy: ((y + dy >= 0) & (y + dy < NY)).astype(F32) for dy in (-1, 0, 1)}


def store_reciprocals(rwt_ref, w_ref, iy):
    lane = lane_iota(ROWS)
    iz = {dz: ((lane + dz >= 0) & (lane + dz < CZ)).astype(F32) for dz in (-1, 0, 1)}
    for case, dxs in enumerate(((0, 1), (-1, 0, 1), (-1, 0))):
        total = jnp.zeros((ROWS, CZ), F32)
        for dy in (-1, 0, 1):
            part = jnp.zeros((ROWS, CZ), F32)
            for dz in (-1, 0, 1):
                w = w_ref[(dxs[0] + 1) * 9 + (dy + 1) * 3 + dz + 1]
                for dx in dxs[1:]:
                    w = w + w_ref[(dx + 1) * 9 + (dy + 1) * 3 + dz + 1]
                part = part + w * iz[dz]
            total = total + part * iy[dy]
        rwt_ref[case] = jnp.where(total > 0.0, iy[0] / jnp.where(total > 0.0, total, 1.0), 0.0)


def on_grid(x):
    return jnp.where((x >= 0) & (x < NX), jnp.float32(1.0), jnp.float32(0.0))


def brick_flags(f1_rows, f0_rows):
    low = sub_iota(8) < 4
    halves = [jnp.where(low, rows[0:1], rows[1:2]) for rows in (f1_rows, f0_rows)]
    return jnp.concatenate(halves, axis=0)


def stiffness_plane(planes, flags, x, inside_y, rwt_ref, w_ref, lane):
    num = filter_plane(planes, w_ref, lane, 1)
    inside = on_grid(x)
    rwt = rwt_ref[jnp.where(x == 0, 0, jnp.where(x == NX - 1, 2, 1))] * inside
    smooth = num * rwt
    sq = flags * (smooth * smooth)
    stiff = (inside_y * inside) * (EMIN + (sq * smooth) * (1.0 - EMIN))
    return stiff, (-3.0 * (1.0 - EMIN)) * sq * rwt


def add_moments(sums, fs, gs, outs):
    m0, m1, m2, m3 = sums
    for f, g, out in zip(fs, gs, outs):
        f, g, out = f[0:8], g[0:8], out[0:8]
        m0, m1, m2, m3 = m0 + f * f, m1 + f * g, m2 + g * g, m3 + g * out
    return m0, m1, m2, m3


def inner_kernel(
    off_ref, dext_ref, fext_ref, w_ref, s_ref, coef_ref, g_ref, sums_ref, rwt_ref
):
    gx, gy = lax.axis_index(GX), lax.axis_index(GY)
    lane = lane_iota(ROWS)
    iy = grid_y(gy)
    store_weights(off_ref, w_ref)
    store_reciprocals(rwt_ref, w_ref, iy)

    def smooth_step(p, _):
        x = p + 1
        planes = [dext_ref[p], dext_ref[p + 1], dext_ref[p + 2]]
        flags = brick_flags(fext_ref[1, x, 11:13], fext_ref[0, x, 11:13])
        s_ref[p], coef_ref[p] = stiffness_plane(
            planes, flags, gx * CX + x, iy[0], rwt_ref, w_ref, lane
        )
        return 0

    lax.fori_loop(0, CX - 2, smooth_step, 0, unroll=UNROLL[0])

    def image_step(q, _):
        outs = image_plane(
            lambda c, k: fext_ref[c, q + 2 + k], s_ref[q], s_ref[q + 1], s_ref[q + 2], lane
        )
        for c in range(3):
            g_ref[c, q] = outs[c] * iy[0]
        return 0

    lax.fori_loop(0, CX - 4, image_step, 0, unroll=UNROLL[1])

    def moment_step(t, sums):
        outs = image_plane(
            lambda c, k: g_ref[c, t + 1 + k], s_ref[t + 1], s_ref[t + 2], s_ref[t + 3], lane
        )
        fs = [fext_ref[c, t + 3] for c in range(3)]
        return add_moments(sums, fs, [g_ref[c, t + 1] for c in range(3)], outs)

    zero = jnp.zeros((8, CZ), F32)
    sums = lax.fori_loop(0, CX - 6, moment_step, (zero,) * 4, unroll=UNROLL[2])
    for k in range(4):
        sums_ref[k] = sums[k]


def rim_kernel(
    w_in, dext_ref, fext_ref, first_in, second_in, s_in_ref, g_in_ref, sums_ref, rwt_ref,
    g_ref, coef_ref, f_rim_ref, mom_ref,
    d2_ref, f2_ref, s2_ref, g2_ref, w_ref, sem,
):
    w_copy = pltpu.make_async_copy(w_in, w_ref, sem)
    w_copy.start()
    gx, gy = lax.axis_index(GX), lax.axis_index(GY)
    lane = lane_iota(ROWS)
    iy = grid_y(gy)
    d2_ref[0, 4:6] = dext_ref[0:2]
    d2_ref[1, 0:2] = dext_ref[14:16]
    s2_ref[0, 4:7] = s_in_ref[0:3]
    s2_ref[1, 0:3] = s_in_ref[11:14]
    for c in range(3):
        f2_ref[c, 0, 3:6] = fext_ref[c, 0:3]
        f2_ref[c, 1, 0:3] = fext_ref[c, 13:16]
        g2_ref[c, 0, 4:6] = g_in_ref[c, 0:2]
        g2_ref[c, 1, 0:2] = g_in_ref[c, 10:12]

    odd = jnp.full((ROWS, CZ), is_odd(gx), jnp.int32) == 1
    for k in range(13):
        one, two = first_in[k], second_in[k]
        below, above = jnp.where(odd, two, one), jnp.where(odd, one, two)
        if k < 4:
            d2_ref[0, k] = below
            d2_ref[1, 2 + k] = above
            continue
        c, i = (k - 4) // 3, (k - 4) % 3
        f2_ref[c, 0, i] = below
        f2_ref[c, 1, 3 + i] = above
        if i >= 1:
            f_rim_ref[c, 0, i - 1] = below
        if i <= 1:
            f_rim_ref[c, 1, i] = above

    w_copy.wait()

    def smooth_step(i, _):
        side, m = lax.shift_right_logical(i, 2), lax.bitwise_and(i, 3)
        planes = [d2_ref[side, m + k] for k in range(3)]
        flags = brick_flags(f2_ref[1, side, m + 2 * side, 11:13], f2_ref[0, side, m + 2 * side, 11:13])
        s2_ref[side, m + 3 * side], coef_ref[side, m] = stiffness_plane(
            planes, flags, gx * CX + m - 3 + 18 * side, iy[0], rwt_ref, w_ref, lane
        )
        return 0

    lax.fori_loop(0, 8, smooth_step, 0, unroll=UNROLL[3])

    def image_step(i, _):
        side, m = lax.shift_right_logical(i, 2), lax.bitwise_and(i, 3)
        n = m + side
        outs = image_plane(
            lambda c, k: f2_ref[c, side, m + 1 + k],
            s2_ref[side, n], s2_ref[side, n + 1], s2_ref[side, n + 2], lane,
        )
        inside = iy[0] * on_grid(gx * CX + m - 2 + 16 * side)
        for c in range(3):
            g = outs[c] * inside
            g_ref[c, side, m] = g
            g2_ref[c, side, m + 2 * side] = g
        return 0

    lax.fori_loop(0, 8, image_step, 0, unroll=UNROLL[4])

    def moment_step(m, sums):
        for side in range(2):
            q = m + 2 - side
            n = m + 3 - 2 * side
            outs = image_plane(
                lambda c, k: g2_ref[c, side, q + k],
                s2_ref[side, n - 1], s2_ref[side, n], s2_ref[side, n + 1], lane,
            )
            fs = [f2_ref[c, side, m + 3 - 3 * side] for c in range(3)]
            sums = add_moments(sums, fs, [g2_ref[c, side, q] for c in range(3)], outs)
        return sums

    sums = lax.fori_loop(0, 3, moment_step, tuple(sums_ref[k] for k in range(4)), unroll=UNROLL[5])
    at = lax.broadcasted_iota(jnp.int32, (1, 128), 1)
    line = jnp.zeros((1, 128), F32)
    for k in range(4):
        total = jnp.sum(jnp.sum(sums[k], axis=0, keepdims=True), axis=1, keepdims=True)
        line = jnp.where(at == k, total, line)
    mom_ref[...] = line


def last_kernel(
    w_in, fext_ref, f_rim_ref, g_in_ref, g_rim_ref, coef_in_ref, coef_rim_ref, mom_ref,
    u_hbm, sens_hbm,
    u_ref, sh_ref, coef_ref, own_ref, sens_ref, w_ref, sem,
):
    w_copy = pltpu.make_async_copy(w_in, w_ref, sem.at[3])
    w_copy.start()
    lane = lane_iota(ROWS)
    line = jnp.sum(mom_ref[...], axis=0, keepdims=True)
    at = lax.broadcasted_iota(jnp.int32, (1, 128), 1)
    m0, m1, m2, m3 = (
        jnp.sum(jnp.where(at == k, line, 0.0), axis=1, keepdims=True) for k in range(4)
    )
    s1 = m0 / m1
    rr = m0 - 2.0 * s1 * m1 + s1 * s1 * m2
    grow = 1.0 + rr / m0
    s2 = rr / (grow * grow * m1 - 2.0 * grow * s1 * m2 + s1 * s1 * m3)
    alpha = jnp.broadcast_to(s1 + s2 * grow, (ROWS, CZ))
    beta = jnp.broadcast_to(-s1 * s2, (ROWS, CZ))

    def u_plane(q, fs, gs):
        us = [alpha * f + beta * g for f, g in zip(fs, gs)]
        for c in range(3):
            u_ref[c, q] = us[c]
        return us

    def u_step(k, _):
        us = u_plane(k + 4, [fext_ref[c, k + 2] for c in range(3)], [g_in_ref[c, k] for c in range(3)])
        for c in range(3):
            own_ref[c, k + 2] = us[c][0:8]
        return 0

    lax.fori_loop(0, CX - 4, u_step, 0, unroll=4)
    for x in (0, 1, 14, 15):
        side, m = (0, x + 2) if x < 8 else (1, x - 14)
        us = u_plane(
            x + 2, [fext_ref[c, x] for c in range(3)], [g_rim_ref[c, side, m] for c in range(3)]
        )
        for c in range(3):
            own_ref[c, x] = us[c][0:8]
    u_copy = pltpu.make_async_copy(own_ref, u_hbm, sem.at[0])
    u_copy.start()
    for q, side, i in ((0, 0, 0), (1, 0, 1), (18, 1, 0), (19, 1, 1)):
        u_plane(
            q,
            [f_rim_ref[c, side, i] for c in range(3)],
            [g_rim_ref[c, side, i + 2 * side] for c in range(3)],
        )
    coef_ref[0:2] = coef_rim_ref[0, 2:4]
    coef_ref[2:16] = coef_in_ref[...]
    coef_ref[16:18] = coef_rim_ref[1, 0:2]

    def share_step(r, _):
        ex = ey = ez = e0 = None
        for c in range(3):
            v = u_ref[c, r + 1]
            ax, bx = v - u_ref[c, r + 2], v - u_ref[c, r]
            ay, az = v - yp(v), v - zp(v, lane)
            tx, ty, tz, t0 = ax * ax + bx * bx, ay * ay, az * az, v * v
            if c == 0:
                tx = tx + tx
            elif c == 1:
                ty = ty + ty
            else:
                tz, t0 = tz + tz, t0 + t0
            ex = tx if ex is None else ex + tx
            ey = ty if ey is None else ey + ty
            ez = tz if ez is None else ez + tz
            e0 = t0 if e0 is None else e0 + t0
        energy = 0.5 * (ex + (ey + ym(ey)) + (ez + zm(ez, lane, e0)))
        sh_ref[r] = coef_ref[r] * energy
        return 0

    lax.fori_loop(0, CX + 2, share_step, 0, unroll=UNROLL[6])

    def out_step(x, _):
        planes = [sh_ref[x], sh_ref[x + 1], sh_ref[x + 2]]
        sens_ref[x] = filter_plane(planes, w_ref, lane, -1)[0:8]
        return 0

    w_copy.wait()
    half = CX // 2
    copies = [u_copy]
    for k in range(2):
        lax.fori_loop(k * half, (k + 1) * half, out_step, 0, unroll=UNROLL[7])
        part = pl.ds(k * half, half)
        copies.append(pltpu.make_async_copy(sens_ref.at[part], sens_hbm.at[part], sem.at[1 + k]))
        copies[-1].start()
    for copy in copies:
        copy.wait()


VMEM = pl.BlockSpec(memory_space=pltpu.VMEM)
SMEM = pl.BlockSpec(memory_space=pltpu.SMEM)


def f32(*shape):
    return jax.ShapeDtypeStruct(shape, F32)


HBM = pl.BlockSpec(memory_space=pltpu.HBM)
ANY = pl.BlockSpec(memory_space=pl.ANY)


def call(kernel, outs, ins, out_specs, scratch, cost=None):
    return pl.pallas_call(
        kernel,
        out_shape=outs,
        in_specs=ins,
        out_specs=out_specs,
        scratch_shapes=scratch,
        cost_estimate=cost,
        compiler_params=pltpu.CompilerParams(vmem_limit_bytes=24 * 1024 * 1024),
    )


def swap(first, second, axes, count):
    got = []
    for slab, start in ((first, 1), (second, 0)):
        pairs = [(i, i + 1) for i in range(start, count - 1, 2)]
        got.append(lax.ppermute(slab, axes, pairs + [(b, a) for a, b in pairs]))
    return got


def spread_sum(line, axes, count):
    lines = jnp.broadcast_to(line, (count, 128))
    return lax.all_to_all(lines, axes, 0, 0, tiled=True)


def body(density, force, brick_ids, offsets):
    ins = (density, force, brick_ids.reshape(1, 512))
    plane = (ROWS, CZ)
    slab_y, slab_x = f32(216, CZ), f32(13, *plane)
    den, f, mask, first, second = call(
        pack_y_kernel,
        (f32(CX, CY, CZ), f32(3, CX, CY, CZ), f32(8, CZ), slab_y, slab_y),
        [HBM, HBM, HBM],
        (VMEM,) * 5,
        [pltpu.VMEM((1, 512), jnp.int32), pltpu.SemaphoreType.DMA((3,))],
    )(*(pltpu.with_memory_space_constraint(a, pltpu.HBM) for a in ins))
    first, second = swap(first, second, GY, DEV_Y)
    dext, fext, first, second = call(
        pack_x_kernel,
        (f32(CX, *plane), f32(3, CX, *plane), slab_x, slab_x),
        [VMEM] * 5,
        (VMEM,) * 4,
        [],
    )(den, f, mask, first, second)
    first, second = swap(first, second, GX, DEV_X)
    w, stiff, coef, image, sums, rwt = call(
        inner_kernel,
        (f32(128), f32(14, *plane), f32(14, *plane), f32(3, 12, *plane), f32(4, 8, CZ), f32(3, *plane)),
        [SMEM, VMEM, VMEM],
        (SMEM,) + (VMEM,) * 5,
        [],
        pl.CostEstimate(flops=8_000_000, bytes_accessed=8_000_000, transcendentals=0),
    )(pltpu.with_memory_space_constraint(offsets.T, pltpu.HBM), dext, fext)
    image_rim, coef_rim, f_rim, line = call(
        rim_kernel,
        (f32(3, 2, 4, *plane), f32(2, 4, *plane), f32(3, 2, 2, *plane), f32(1, 128)),
        [ANY] + [VMEM] * 8,
        (VMEM,) * 4,
        [
            pltpu.VMEM((2, 6, *plane), F32),
            pltpu.VMEM((3, 2, 6, *plane), F32),
            pltpu.VMEM((2, 7, *plane), F32),
            pltpu.VMEM((3, 2, 6, *plane), F32),
            pltpu.SMEM((128,), F32),
            pltpu.SemaphoreType.DMA(()),
        ],
    )(w, dext, fext, first, second, stiff, image, sums, rwt)
    lines = spread_sum(line, ("x", "y"), 32)
    lines = spread_sum(jnp.sum(lines, axis=0, keepdims=True), ("zl", "zh", "c"), 24)
    return call(
        last_kernel,
        (f32(3, CX, CY, CZ), f32(CX, CY, CZ)),
        [ANY] + [VMEM] * 7,
        (HBM, HBM),
        [
            pltpu.VMEM((3, CX + 4, *plane), F32),
            pltpu.VMEM((CX + 2, *plane), F32),
            pltpu.VMEM((CX + 2, *plane), F32),
            pltpu.VMEM((3, CX, CY, CZ), F32),
            pltpu.VMEM((CX, CY, CZ), F32),
            pltpu.SMEM((128,), F32),
            pltpu.SemaphoreType.DMA((4,)),
        ],
    )(w, fext, f_rim, image, image_rim, coef, coef_rim, lines)


def solution(mesh):
    fine = Mesh(mesh.devices.reshape(3, 4, 4, 8, 2), ("zl", "x", "zh", "y", "c"))
    return jax.shard_map(
        body,
        mesh=fine,
        in_specs=(P(GX, GY, None), P(None, GX, GY, None), P(GX, GY, None), P()),
        out_specs=(P(None, GX, GY, None), P(GX, GY, None)),
        check_vma=False,
    )
```

```python
import functools

import jax
import jax.numpy as jnp
import numpy as np
from jax import lax
from jax.experimental import pallas as pl
from jax.experimental.pallas import tpu as pltpu
from jax.sharding import Mesh
from jax.sharding import PartitionSpec as P

EMIN = 0.001
RADIUS = 2.0
REACH = [float(np.float32(RADIUS) - np.float32(np.sqrt(np.float32(s)))) for s in range(4)]

CX, CY, CZ = 16, 8, 256
NX, NY = 192, 512
DEV_X, DEV_Y = 12, 64
GX, GY = ("zl", "x"), ("zh", "y", "c")
ROWS = 16
F32 = jnp.float32
UNROLL = (7, 4, 5, 8, 4, 3, 9, 8)


def sub_iota(rows):
    return lax.broadcasted_iota(jnp.int32, (rows, CZ), 0)


def lane_iota(rows):
    return lax.broadcasted_iota(jnp.int32, (rows, CZ), 1)


def roll(v, shift, axis):
    return pltpu.roll(v, shift % v.shape[axis], axis)


def yp(v):
    return roll(v, -1, 0)


def ym(v):
    return roll(v, 1, 0)


def zp(v, lane, fill=0.0):
    return jnp.where(lane == CZ - 1, fill, roll(v, -1, 1))


def zm(v, lane, fill=0.0):
    return jnp.where(lane == 0, fill, roll(v, 1, 1))


def is_odd(at):
    return lax.bitwise_and(at, 1)


def store_weights(off_ref, w_ref):
    for i in range(27):
        w_ref[i] = jnp.float32(0.0)
    for j in range(off_ref.shape[1]):
        dx, dy, dz = off_ref[0, j], off_ref[1, j], off_ref[2, j]
        s = dx * dx + dy * dy + dz * dz
        w = jnp.where(
            s == 0,
            jnp.float32(REACH[0]),
            jnp.where(
                s == 1,
                jnp.float32(REACH[1]),
                jnp.where(s == 2, jnp.float32(REACH[2]), jnp.float32(REACH[3])),
            ),
        )
        w_ref[(dx + 1) * 9 + (dy + 1) * 3 + dz + 1] = w


def pack_y_kernel(
    den_hbm, f_hbm, ids_hbm, den_ref, f_ref, m_ref, first_ref, second_ref, ids_ref, sem
):
    copies = [
        pltpu.make_async_copy(src, dst, sem.at[i])
        for i, (src, dst) in enumerate(((ids_hbm, ids_ref), (den_hbm, den_ref), (f_hbm, f_ref)))
    ]
    for copy in copies:
        copy.start()
    copies[0].wait()
    ids = ids_ref[...]
    row = lax.shift_right_logical(ids, 6)
    col = lax.bitwise_and(ids, 63)
    p = (lax.broadcasted_iota(jnp.int32, (8, 512), 0) == row).astype(jnp.bfloat16)
    q = (
        lax.shift_right_logical(lax.broadcasted_iota(jnp.int32, (CZ, 512), 0), 2) == col
    ).astype(jnp.bfloat16)
    flags = lax.dot_general(p, q, (((1,), (1,)), ((), ())), preferred_element_type=F32)
    m_ref[...] = flags
    copies[1].wait()
    copies[2].wait()
    den = jnp.swapaxes(den_ref[...], 0, 1)
    fs = [jnp.swapaxes(f_ref[c], 0, 1) for c in range(3)]

    odd = jnp.full((CX, CZ), is_odd(lax.axis_index(GY)), jnp.int32) == 1

    def fill(at, lo, hi):
        first_ref[at : at + 16] = jnp.where(odd, hi, lo)
        second_ref[at : at + 16] = jnp.where(odd, lo, hi)

    first_ref[208:216] = flags
    second_ref[208:216] = flags
    for j in range(4):
        fill(16 * j, den[j], den[4 + j])
    for c in range(3):
        for j in range(3):
            fill(64 + 16 * (3 * c + j), fs[c][j], fs[c][5 + j])


def pack_x_kernel(
    den_ref, f_ref, m_ref, first_in, second_in, dext_ref, fext_ref, first_ref, second_ref
):
    odd_y = jnp.full((CX, CZ), is_odd(lax.axis_index(GY)), jnp.int32) == 1

    def below(first, count):
        return jnp.where(odd_y[0:count], second_in[first : first + count], first_in[first : first + count])

    def above(first, count):
        return jnp.where(odd_y[0:count], first_in[first : first + count], second_in[first : first + count])

    def spread_flags(flags, by):
        rows = [flags[2 * bx + by : 2 * bx + by + 1] for bx in range(4)]
        return jnp.concatenate([jnp.broadcast_to(r, (4, CZ)) for r in rows], axis=0)

    def halo_rows(planes):
        return jnp.swapaxes(jnp.stack(planes), 0, 1)

    dext_ref[:, 0:8] = den_ref[...]
    dext_ref[:, 8:16] = halo_rows(
        [above(16 * j, 16) for j in range(4)] + [below(16 * j, 16) for j in range(4)]
    )
    own = m_ref[...]
    flags = (
        [spread_flags(above(208, 8), 0), spread_flags(below(208, 8), 1)],
        [spread_flags(own, 0), spread_flags(own, 1)],
        [jnp.zeros((CX, CZ), F32)] * 2,
    )
    for c in range(3):
        at = [64 + 16 * (3 * c + j) for j in range(3)]
        fext_ref[c, :, 0:8] = f_ref[c]
        fext_ref[c, :, 8:16] = halo_rows(
            [above(i, 16) for i in at] + flags[c] + [below(i, 16) for i in at]
        )
    odd_x = is_odd(lax.axis_index(GX))
    sub = sub_iota(8)
    spare = (sub == 2) | (sub == 3)
    for slab, top in ((first_ref, odd_x), (second_ref, 1 - odd_x)):
        near, deep = 13 * top, 2 + 11 * top
        slab[0:4] = dext_ref[pl.ds(12 * top, 4), 0:8]
        slab[13:17] = dext_ref[pl.ds(12 * top, 4), 8:16]
        for c in range(3):
            slab[4 + 3 * c : 7 + 3 * c] = fext_ref[c, pl.ds(near, 3), 0:8]
            slab[17 + 2 * c] = fext_ref[c, 15 * top, 8:16]
            deepest = roll(fext_ref[c, deep, 8:16], 3, 0)
            slab[18 + 2 * c] = jnp.where(spare, deepest, fext_ref[c, 1 + 13 * top, 8:16])


def filter_plane(planes, w_ref, lane, sign, rows=ROWS):
    out = None
    for dz in (-1, 0, 1):
        acc = None
        for dy in (-1, 0, 1):
            t = None
            for dx in (-1, 0, 1):
                w = w_ref[(sign * dx + 1) * 9 + (sign * dy + 1) * 3 + sign * dz + 1]
                term = planes[dx + 1][0 : rows if dy == 0 else ROWS] * w
                t = term if t is None else t + term
            if dy == 1:
                t = yp(t)
            elif dy == -1:
                t = ym(t)
            t = t[0:rows]
            acc = t if acc is None else acc + t
        if dz == 1:
            acc = zp(acc, lane)
        elif dz == -1:
            acc = zm(acc, lane)
        out = acc if out is None else out + acc
    return out


def image_plane(load, s_m, s_0, s_p, lane, rows=ROWS):
    py = 0.5 * (s_0 + yp(s_0))
    s_m, s_0, s_p, lane = s_m[0:rows], s_0[0:rows], s_p[0:rows], lane[0:rows]
    px, mx = 0.5 * (s_0 + s_p), 0.5 * (s_0 + s_m)
    pz = 0.5 * (s_0 + zp(s_0, lane))
    half = -0.5 * s_0
    outs = []
    for c in range(3):
        v = load(c, 0)
        fy = py * (v - yp(v))
        fy = fy[0:rows] - ym(fy)[0:rows]
        v = v[0:rows]
        fx = px * (v - load(c, 1)[0:rows]) + mx * (v - load(c, -1)[0:rows])
        fz = pz * (v - zp(v, lane))
        fz = fz - zm(fz, lane, half * v)
        outs.append(fx + fy + fz + (fx, fy, fz)[c])
    return outs


def grid_y(gy):
    sub = sub_iota(ROWS)
    y = jnp.where(sub < 12, sub, sub - 16) + gy * CY
    return {dy: ((y + dy >= 0) & (y + dy < NY)).astype(F32) for dy in (-1, 0, 1)}


def store_reciprocals(rwt_ref, w_ref, iy):
    lane = lane_iota(ROWS)
    iz = {dz: ((lane + dz >= 0) & (lane + dz < CZ)).astype(F32) for dz in (-1, 0, 1)}
    for case, dxs in enumerate(((0, 1), (-1, 0, 1), (-1, 0))):
        total = jnp.zeros((ROWS, CZ), F32)
        for dy in (-1, 0, 1):
            part = jnp.zeros((ROWS, CZ), F32)
            for dz in (-1, 0, 1):
                w = w_ref[(dxs[0] + 1) * 9 + (dy + 1) * 3 + dz + 1]
                for dx in dxs[1:]:
                    w = w + w_ref[(dx + 1) * 9 + (dy + 1) * 3 + dz + 1]
                part = part + w * iz[dz]
            total = total + part * iy[dy]
        rwt_ref[case] = jnp.where(total > 0.0, iy[0] / jnp.where(total > 0.0, total, 1.0), 0.0)


def on_grid(x):
    return jnp.where((x >= 0) & (x < NX), jnp.float32(1.0), jnp.float32(0.0))


def brick_flags(f1_rows, f0_rows):
    low = sub_iota(8) < 4
    halves = [jnp.where(low, rows[0:1], rows[1:2]) for rows in (f1_rows, f0_rows)]
    return jnp.concatenate(halves, axis=0)


def stiffness_plane(planes, flags, x, inside_y, rwt_ref, w_ref, lane):
    num = filter_plane(planes, w_ref, lane, 1)
    inside = on_grid(x)
    rwt = rwt_ref[jnp.where(x == 0, 0, jnp.where(x == NX - 1, 2, 1))] * inside
    smooth = num * rwt
    sq = flags * (smooth * smooth)
    stiff = (inside_y * inside) * (EMIN + (sq * smooth) * (1.0 - EMIN))
    return stiff, (-3.0 * (1.0 - EMIN)) * sq * rwt


def add_moments(sums, fs, gs, outs):
    m0, m1, m2, m3 = sums
    for f, g, out in zip(fs, gs, outs):
        f, g, out = f[0:8], g[0:8], out[0:8]
        m0, m1, m2, m3 = m0 + f * f, m1 + f * g, m2 + g * g, m3 + g * out
    return m0, m1, m2, m3


def inner_kernel(
    off_ref, dext_ref, fext_ref, w_ref, s_ref, coef_ref, g_ref, sums_ref, rwt_ref
):
    gx, gy = lax.axis_index(GX), lax.axis_index(GY)
    lane = lane_iota(ROWS)
    iy = grid_y(gy)
    store_weights(off_ref, w_ref)
    store_reciprocals(rwt_ref, w_ref, iy)

    def smooth_step(p, _):
        x = p + 1
        planes = [dext_ref[p], dext_ref[p + 1], dext_ref[p + 2]]
        flags = brick_flags(fext_ref[1, x, 11:13], fext_ref[0, x, 11:13])
        s_ref[p], coef_ref[p] = stiffness_plane(
            planes, flags, gx * CX + x, iy[0], rwt_ref, w_ref, lane
        )
        return 0

    lax.fori_loop(0, CX - 2, smooth_step, 0, unroll=UNROLL[0])

    def image_step(q, _):
        outs = image_plane(
            lambda c, k: fext_ref[c, q + 2 + k], s_ref[q], s_ref[q + 1], s_ref[q + 2], lane
        )
        for c in range(3):
            g_ref[c, q] = outs[c] * iy[0]
        return 0

    lax.fori_loop(0, CX - 4, image_step, 0, unroll=UNROLL[1])

    def moment_step(t, sums):
        outs = image_plane(
            lambda c, k: g_ref[c, t + 1 + k], s_ref[t + 1], s_ref[t + 2], s_ref[t + 3], lane, 8
        )
        fs = [fext_ref[c, t + 3] for c in range(3)]
        return add_moments(sums, fs, [g_ref[c, t + 1] for c in range(3)], outs)

    zero = jnp.zeros((8, CZ), F32)
    sums = lax.fori_loop(0, CX - 6, moment_step, (zero,) * 4, unroll=UNROLL[2])
    for k in range(4):
        sums_ref[k] = sums[k]


def rim_kernel(
    w_in, dext_ref, fext_ref, first_in, second_in, s_in_ref, g_in_ref, sums_ref, rwt_ref,
    g_ref, coef_ref, f_rim_ref, mom_ref,
    d2_ref, f2_ref, s2_ref, g2_ref, w_ref, sem,
):
    w_copy = pltpu.make_async_copy(w_in, w_ref, sem)
    w_copy.start()
    gx, gy = lax.axis_index(GX), lax.axis_index(GY)
    lane = lane_iota(ROWS)
    iy = grid_y(gy)
    d2_ref[0, 4:6] = dext_ref[0:2]
    d2_ref[1, 0:2] = dext_ref[14:16]
    s2_ref[0, 4:7] = s_in_ref[0:3]
    s2_ref[1, 0:3] = s_in_ref[11:14]
    for c in range(3):
        f2_ref[c, 0, 3:6] = fext_ref[c, 0:3]
        f2_ref[c, 1, 0:3] = fext_ref[c, 13:16]
        g2_ref[c, 0, 4:6] = g_in_ref[c, 0:2]
        g2_ref[c, 1, 0:2] = g_in_ref[c, 10:12]

    odd = jnp.full((8, CZ), is_odd(gx), jnp.int32) == 1
    own_rows, halo_rows = slice(0, 8), slice(8, 16)
    for k in range(23):
        one, two = first_in[k], second_in[k]
        sides = jnp.where(odd, two, one), jnp.where(odd, one, two)
        if k < 4 or 13 <= k < 17:
            rows, i = (own_rows, k) if k < 4 else (halo_rows, k - 13)
            for side in range(2):
                d2_ref[side, i + 2 * side, rows] = sides[side]
            continue
        for side in range(2):
            if k < 13:
                c, rows = (k - 4) // 3, own_rows
                parts = (((k - 4) % 3, sides[side]),)
            else:
                c, rows = (k - 17) // 2, halo_rows
                order = (0, 1, 2) if side else (2, 1, 0)
                if (k - 17) % 2 == 0:
                    parts = ((order[0], sides[side]),)
                else:
                    parts = ((order[1], sides[side]), (order[2], roll(sides[side], -3, 0)))
            for i, part in parts:
                f2_ref[c, side, i + 3 * side, rows] = part
                if i + side in (1, 2) and i - 1 + side >= 0:
                    f_rim_ref[c, side, i - 1 + side, rows] = part

    w_copy.wait()

    def smooth_step(i, _):
        side, m = lax.shift_right_logical(i, 2), lax.bitwise_and(i, 3)
        planes = [d2_ref[side, m + k] for k in range(3)]
        at = jnp.where(side == 0, jnp.maximum(m, 2), jnp.minimum(m + 2, 3))
        flags = brick_flags(f2_ref[1, side, at, 11:13], f2_ref[0, side, at, 11:13])
        s2_ref[side, m + 3 * side], coef_ref[side, m] = stiffness_plane(
            planes, flags, gx * CX + m - 3 + 18 * side, iy[0], rwt_ref, w_ref, lane
        )
        return 0

    lax.fori_loop(0, 8, smooth_step, 0, unroll=UNROLL[3])

    def image_step(i, _):
        side, m = lax.shift_right_logical(i, 2), lax.bitwise_and(i, 3)
        n = m + side
        outs = image_plane(
            lambda c, k: f2_ref[c, side, m + 1 + k],
            s2_ref[side, n], s2_ref[side, n + 1], s2_ref[side, n + 2], lane,
        )
        inside = iy[0] * on_grid(gx * CX + m - 2 + 16 * side)
        for c in range(3):
            g = outs[c] * inside
            g_ref[c, side, m] = g
            g2_ref[c, side, m + 2 * side] = g
        return 0

    lax.fori_loop(0, 8, image_step, 0, unroll=UNROLL[4])

    def moment_step(m, sums):
        for side in range(2):
            q = m + 2 - side
            n = m + 3 - 2 * side
            outs = image_plane(
                lambda c, k: g2_ref[c, side, q + k],
                s2_ref[side, n - 1], s2_ref[side, n], s2_ref[side, n + 1], lane, 8,
            )
            fs = [f2_ref[c, side, m + 3 - 3 * side] for c in range(3)]
            sums = add_moments(sums, fs, [g2_ref[c, side, q] for c in range(3)], outs)
        return sums

    sums = lax.fori_loop(0, 3, moment_step, tuple(sums_ref[k] for k in range(4)), unroll=UNROLL[5])
    at = lax.broadcasted_iota(jnp.int32, (1, 128), 1)
    line = jnp.zeros((1, 128), F32)
    for k in range(4):
        total = jnp.sum(jnp.sum(sums[k], axis=0, keepdims=True), axis=1, keepdims=True)
        line = jnp.where(at == k, total, line)
    mom_ref[...] = line


def last_kernel(
    w_in, fext_ref, f_rim_ref, g_in_ref, g_rim_ref, coef_in_ref, coef_rim_ref, mom_ref,
    u_hbm, sens_hbm,
    u_ref, sh_ref, coef_ref, own_ref, sens_ref, w_ref, sem,
):
    w_copy = pltpu.make_async_copy(w_in, w_ref, sem.at[3])
    w_copy.start()
    lane = lane_iota(ROWS)
    line = jnp.sum(mom_ref[...], axis=0, keepdims=True)
    at = lax.broadcasted_iota(jnp.int32, (1, 128), 1)
    m0, m1, m2, m3 = (
        jnp.sum(jnp.where(at == k, line, 0.0), axis=1, keepdims=True) for k in range(4)
    )
    inverse = 1.0 / m1
    s1 = m0 * inverse
    grow = s1 * m2 * inverse
    rr = m0 * (grow - 1.0)
    s2 = rr / (grow * grow * m1 - 2.0 * grow * s1 * m2 + s1 * s1 * m3)
    alpha = jnp.broadcast_to(s1 + s2 * grow, (ROWS, CZ))
    beta = jnp.broadcast_to(-s1 * s2, (ROWS, CZ))

    def u_plane(q, fs, gs):
        us = [alpha * f + beta * g for f, g in zip(fs, gs)]
        for c in range(3):
            u_ref[c, q] = us[c]
        return us

    def u_step(k, _):
        us = u_plane(k + 4, [fext_ref[c, k + 2] for c in range(3)], [g_in_ref[c, k] for c in range(3)])
        for c in range(3):
            own_ref[c, k + 2] = us[c][0:8]
        return 0

    lax.fori_loop(0, CX - 4, u_step, 0, unroll=4)
    for x in (0, 1, 14, 15):
        side, m = (0, x + 2) if x < 8 else (1, x - 14)
        us = u_plane(
            x + 2, [fext_ref[c, x] for c in range(3)], [g_rim_ref[c, side, m] for c in range(3)]
        )
        for c in range(3):
            own_ref[c, x] = us[c][0:8]
    u_copy = pltpu.make_async_copy(own_ref, u_hbm, sem.at[0])
    u_copy.start()
    for q, side, i in ((0, 0, 0), (1, 0, 1), (18, 1, 0), (19, 1, 1)):
        u_plane(
            q,
            [f_rim_ref[c, side, i] for c in range(3)],
            [g_rim_ref[c, side, i + 2 * side] for c in range(3)],
        )
    coef_ref[0:2] = coef_rim_ref[0, 2:4]
    coef_ref[2:16] = coef_in_ref[...]
    coef_ref[16:18] = coef_rim_ref[1, 0:2]

    def share_step(r, _):
        ex = ey = ez = e0 = None
        for c in range(3):
            v = u_ref[c, r + 1]
            ax, bx = v - u_ref[c, r + 2], v - u_ref[c, r]
            ay, az = v - yp(v), v - zp(v, lane)
            tx, ty, tz, t0 = ax * ax + bx * bx, ay * ay, az * az, v * v
            if c == 0:
                tx = tx + tx
            elif c == 1:
                ty = ty + ty
            else:
                tz, t0 = tz + tz, t0 + t0
            ex = tx if ex is None else ex + tx
            ey = ty if ey is None else ey + ty
            ez = tz if ez is None else ez + tz
            e0 = t0 if e0 is None else e0 + t0
        energy = 0.5 * (ex + (ey + ym(ey)) + (ez + zm(ez, lane, e0)))
        sh_ref[r] = coef_ref[r] * energy
        return 0

    lax.fori_loop(0, CX + 2, share_step, 0, unroll=UNROLL[6])

    def out_step(x, _):
        planes = [sh_ref[x], sh_ref[x + 1], sh_ref[x + 2]]
        sens_ref[x] = filter_plane(planes, w_ref, lane[0:8], -1, 8)
        return 0

    w_copy.wait()
    half = CX // 2
    copies = [u_copy]
    for k in range(2):
        lax.fori_loop(k * half, (k + 1) * half, out_step, 0, unroll=UNROLL[7])
        part = pl.ds(k * half, half)
        copies.append(pltpu.make_async_copy(sens_ref.at[part], sens_hbm.at[part], sem.at[1 + k]))
        copies[-1].start()
    for copy in copies:
        copy.wait()


VMEM = pl.BlockSpec(memory_space=pltpu.VMEM)
SMEM = pl.BlockSpec(memory_space=pltpu.SMEM)


def f32(*shape):
    return jax.ShapeDtypeStruct(shape, F32)


HBM = pl.BlockSpec(memory_space=pltpu.HBM)
ANY = pl.BlockSpec(memory_space=pl.ANY)


def call(kernel, outs, ins, out_specs, scratch, cost=None):
    return pl.pallas_call(
        kernel,
        out_shape=outs,
        in_specs=ins,
        out_specs=out_specs,
        scratch_shapes=scratch,
        cost_estimate=cost,
        compiler_params=pltpu.CompilerParams(vmem_limit_bytes=24 * 1024 * 1024),
    )


def swap(first, second, axes, count):
    got = []
    for slab, start in ((first, 1), (second, 0)):
        pairs = [(i, i + 1) for i in range(start, count - 1, 2)]
        got.append(lax.ppermute(slab, axes, pairs + [(b, a) for a, b in pairs]))
    return got


def spread_sum(line, axes, count):
    lines = jnp.broadcast_to(line, (count, 128))
    return lax.all_to_all(lines, axes, 0, 0, tiled=True)


def body(density, force, brick_ids, offsets):
    ins = (density, force, brick_ids.reshape(1, 512))
    plane = (ROWS, CZ)
    slab_y, slab_x = f32(216, CZ), f32(23, 8, CZ)
    den, f, mask, first, second = call(
        pack_y_kernel,
        (f32(CX, CY, CZ), f32(3, CX, CY, CZ), f32(8, CZ), slab_y, slab_y),
        [HBM, HBM, HBM],
        (VMEM,) * 5,
        [pltpu.VMEM((1, 512), jnp.int32), pltpu.SemaphoreType.DMA((3,))],
    )(*(pltpu.with_memory_space_constraint(a, pltpu.HBM) for a in ins))
    first, second = swap(first, second, GY, DEV_Y)
    dext, fext, first, second = call(
        pack_x_kernel,
        (f32(CX, *plane), f32(3, CX, *plane), slab_x, slab_x),
        [VMEM] * 5,
        (VMEM,) * 4,
        [],
    )(den, f, mask, first, second)
    first, second = swap(first, second, GX, DEV_X)
    w, stiff, coef, image, sums, rwt = call(
        inner_kernel,
        (f32(128), f32(14, *plane), f32(14, *plane), f32(3, 12, *plane), f32(4, 8, CZ), f32(3, *plane)),
        [SMEM, VMEM, VMEM],
        (SMEM,) + (VMEM,) * 5,
        [],
        pl.CostEstimate(flops=8_000_000, bytes_accessed=8_000_000, transcendentals=0),
    )(pltpu.with_memory_space_constraint(offsets.T, pltpu.HBM), dext, fext)
    image_rim, coef_rim, f_rim, line = call(
        rim_kernel,
        (f32(3, 2, 4, *plane), f32(2, 4, *plane), f32(3, 2, 2, *plane), f32(1, 128)),
        [ANY] + [VMEM] * 8,
        (VMEM,) * 4,
        [
            pltpu.VMEM((2, 6, *plane), F32),
            pltpu.VMEM((3, 2, 6, *plane), F32),
            pltpu.VMEM((2, 7, *plane), F32),
            pltpu.VMEM((3, 2, 6, *plane), F32),
            pltpu.SMEM((128,), F32),
            pltpu.SemaphoreType.DMA(()),
        ],
    )(w, dext, fext, first, second, stiff, image, sums, rwt)
    lines = spread_sum(line, ("zl", "zh", "c"), 24)
    lines = spread_sum(jnp.sum(lines, axis=0, keepdims=True), ("x", "y"), 32)
    return call(
        last_kernel,
        (f32(3, CX, CY, CZ), f32(CX, CY, CZ)),
        [ANY] + [VMEM] * 7,
        (HBM, HBM),
        [
            pltpu.VMEM((3, CX + 4, *plane), F32),
            pltpu.VMEM((CX + 2, *plane), F32),
            pltpu.VMEM((CX + 2, *plane), F32),
            pltpu.VMEM((3, CX, CY, CZ), F32),
            pltpu.VMEM((CX, CY, CZ), F32),
            pltpu.SMEM((128,), F32),
            pltpu.SemaphoreType.DMA((4,)),
        ],
    )(w, fext, f_rim, image, image_rim, coef, coef_rim, lines)


def solution(mesh):
    fine = Mesh(mesh.devices.reshape(3, 4, 4, 8, 2), ("zl", "x", "zh", "y", "c"))
    return jax.shard_map(
        body,
        mesh=fine,
        in_specs=(P(GX, GY, None), P(None, GX, GY, None), P(GX, GY, None), P()),
        out_specs=(P(None, GX, GY, None), P(GX, GY, None)),
        check_vma=False,
    )
```

```python
import functools

import jax
import jax.numpy as jnp
import numpy as np
from jax import lax
from jax.experimental import pallas as pl
from jax.experimental.pallas import tpu as pltpu
from jax.sharding import Mesh
from jax.sharding import PartitionSpec as P

EMIN = 0.001
RADIUS = 2.0
REACH = [float(np.float32(RADIUS) - np.float32(np.sqrt(np.float32(s)))) for s in range(4)]

CX, CY, CZ = 16, 8, 256
NX, NY = 192, 512
DEV_X, DEV_Y = 12, 64
GX, GY = ("zl", "x"), ("zh", "y", "c")
ROWS = 16
F32 = jnp.float32
UNROLL = (7, 4, 5, 4, 4, 3, 9, 8)


def sub_iota(rows):
    return lax.broadcasted_iota(jnp.int32, (rows, CZ), 0)


def lane_iota(rows):
    return lax.broadcasted_iota(jnp.int32, (rows, CZ), 1)


def roll(v, shift, axis):
    return pltpu.roll(v, shift % v.shape[axis], axis)


def yp(v):
    return roll(v, -1, 0)


def ym(v):
    return roll(v, 1, 0)


def zp(v, lane, fill=0.0):
    return jnp.where(lane == CZ - 1, fill, roll(v, -1, 1))


def zm(v, lane, fill=0.0):
    return jnp.where(lane == 0, fill, roll(v, 1, 1))


def is_odd(at):
    return lax.bitwise_and(at, 1)


def partner_side(at, second):
    return 1 - is_odd(at) if second else is_odd(at)


def store_weights(off_ref, w_ref):
    for i in range(27):
        w_ref[i] = jnp.float32(0.0)
    for j in range(off_ref.shape[1]):
        dx, dy, dz = off_ref[0, j], off_ref[1, j], off_ref[2, j]
        s = dx * dx + dy * dy + dz * dz
        w = jnp.where(
            s == 0,
            jnp.float32(REACH[0]),
            jnp.where(
                s == 1,
                jnp.float32(REACH[1]),
                jnp.where(s == 2, jnp.float32(REACH[2]), jnp.float32(REACH[3])),
            ),
        )
        w_ref[(dx + 1) * 9 + (dy + 1) * 3 + dz + 1] = w


def pack_y_kernel(
    den_hbm, f_hbm, ids_hbm, den_ref, f_ref, m_ref, first_ref, second_ref, ids_ref, sem
):
    copies = [
        pltpu.make_async_copy(src, dst, sem.at[i])
        for i, (src, dst) in enumerate(((ids_hbm, ids_ref), (den_hbm, den_ref), (f_hbm, f_ref)))
    ]
    for copy in copies:
        copy.start()
    copies[0].wait()
    ids = ids_ref[...]
    row = lax.shift_right_logical(ids, 6)
    col = lax.bitwise_and(ids, 63)
    p = (lax.broadcasted_iota(jnp.int32, (8, 512), 0) == row).astype(jnp.bfloat16)
    q = (
        lax.shift_right_logical(lax.broadcasted_iota(jnp.int32, (CZ, 512), 0), 2) == col
    ).astype(jnp.bfloat16)
    flags = lax.dot_general(p, q, (((1,), (1,)), ((), ())), preferred_element_type=F32)
    m_ref[...] = flags
    copies[1].wait()
    copies[2].wait()
    den = jnp.swapaxes(den_ref[...], 0, 1)
    fs = [jnp.swapaxes(f_ref[c], 0, 1) for c in range(3)]

    odd = jnp.full((CX, CZ), is_odd(lax.axis_index(GY)), jnp.int32) == 1

    def fill(at, lo, hi):
        first_ref[at : at + 16] = jnp.where(odd, hi, lo)
        second_ref[at : at + 16] = jnp.where(odd, lo, hi)

    first_ref[208:216] = flags
    second_ref[208:216] = flags
    for j in range(4):
        fill(16 * j, den[j], den[4 + j])
    for c in range(3):
        for j in range(3):
            fill(64 + 16 * (3 * c + j), fs[c][j], fs[c][5 + j])


def pack_x_kernel(
    den_ref, f_ref, m_ref, first_in, second_in, _, dext_ref, fext_ref, first_ref, second_ref
):
    odd_y = jnp.full((CX, CZ), is_odd(lax.axis_index(GY)), jnp.int32) == 1

    def below(first, count):
        return jnp.where(odd_y[0:count], second_in[first : first + count], first_in[first : first + count])

    def above(first, count):
        return jnp.where(odd_y[0:count], first_in[first : first + count], second_in[first : first + count])

    def spread_flags(flags, by):
        rows = [flags[2 * bx + by : 2 * bx + by + 1] for bx in range(4)]
        return jnp.concatenate([jnp.broadcast_to(r, (4, CZ)) for r in rows], axis=0)

    def halo_rows(planes):
        return jnp.swapaxes(jnp.stack(planes), 0, 1)

    dext_ref[:, 0:8] = den_ref[...]
    dext_ref[:, 8:16] = halo_rows(
        [above(16 * j, 16) for j in range(4)] + [below(16 * j, 16) for j in range(4)]
    )
    own = m_ref[...]
    flags = (
        [spread_flags(above(208, 8), 0), spread_flags(below(208, 8), 1)],
        [spread_flags(own, 0), spread_flags(own, 1)],
        [jnp.zeros((CX, CZ), F32)] * 2,
    )
    for c in range(3):
        at = [64 + 16 * (3 * c + j) for j in range(3)]
        fext_ref[c, :, 0:8] = f_ref[c]
        fext_ref[c, :, 8:16] = halo_rows(
            [above(i, 16) for i in at] + flags[c] + [below(i, 16) for i in at]
        )
    odd_x = is_odd(lax.axis_index(GX))
    sub = sub_iota(8)
    spare = (sub == 2) | (sub == 3)
    for slab, top in ((first_ref, odd_x), (second_ref, 1 - odd_x)):
        near, deep = 13 * top, 2 + 11 * top
        slab[0:4] = dext_ref[pl.ds(12 * top, 4), 0:8]
        slab[13:17] = dext_ref[pl.ds(12 * top, 4), 8:16]
        for c in range(3):
            slab[4 + 3 * c : 7 + 3 * c] = fext_ref[c, pl.ds(near, 3), 0:8]
            slab[17 + 2 * c] = fext_ref[c, 15 * top, 8:16]
            deepest = roll(fext_ref[c, deep, 8:16], 3, 0)
            slab[18 + 2 * c] = jnp.where(spare, deepest, fext_ref[c, 1 + 13 * top, 8:16])


def filter_plane(planes, w_ref, lane, sign, rows=ROWS):
    out = None
    for dz in (-1, 0, 1):
        acc = None
        for dy in (-1, 0, 1):
            t = None
            for dx in (-1, 0, 1):
                w = w_ref[(sign * dx + 1) * 9 + (sign * dy + 1) * 3 + sign * dz + 1]
                term = planes[dx + 1][0 : rows if dy == 0 else ROWS] * w
                t = term if t is None else t + term
            if dy == 1:
                t = yp(t)
            elif dy == -1:
                t = ym(t)
            t = t[0:rows]
            acc = t if acc is None else acc + t
        if dz == 1:
            acc = zp(acc, lane)
        elif dz == -1:
            acc = zm(acc, lane)
        out = acc if out is None else out + acc
    return out


def image_plane(load, s_m, s_0, s_p, lane, rows=ROWS):
    py = 0.5 * (s_0 + yp(s_0))
    s_m, s_0, s_p, lane = s_m[0:rows], s_0[0:rows], s_p[0:rows], lane[0:rows]
    px, mx = 0.5 * (s_0 + s_p), 0.5 * (s_0 + s_m)
    pz = 0.5 * (s_0 + zp(s_0, lane))
    half = -0.5 * s_0
    outs = []
    for c in range(3):
        v = load(c, 0)
        fy = py * (v - yp(v))
        fy = fy[0:rows] - ym(fy)[0:rows]
        v = v[0:rows]
        fx = px * (v - load(c, 1)[0:rows]) + mx * (v - load(c, -1)[0:rows])
        fz = pz * (v - zp(v, lane))
        fz = fz - zm(fz, lane, half * v)
        outs.append(fx + fy + fz + (fx, fy, fz)[c])
    return outs


def grid_y(gy):
    sub = sub_iota(ROWS)
    y = jnp.where(sub < 12, sub, sub - 16) + gy * CY
    return {dy: ((y + dy >= 0) & (y + dy < NY)).astype(F32) for dy in (-1, 0, 1)}


def store_reciprocals(rwt_ref, w_ref, iy):
    lane = lane_iota(ROWS)
    iz = {dz: ((lane + dz >= 0) & (lane + dz < CZ)).astype(F32) for dz in (-1, 0, 1)}
    for case, dxs in enumerate(((0, 1), (-1, 0, 1), (-1, 0))):
        total = jnp.zeros((ROWS, CZ), F32)
        for dy in (-1, 0, 1):
            part = jnp.zeros((ROWS, CZ), F32)
            for dz in (-1, 0, 1):
                w = w_ref[(dxs[0] + 1) * 9 + (dy + 1) * 3 + dz + 1]
                for dx in dxs[1:]:
                    w = w + w_ref[(dx + 1) * 9 + (dy + 1) * 3 + dz + 1]
                part = part + w * iz[dz]
            total = total + part * iy[dy]
        rwt_ref[case] = jnp.where(total > 0.0, iy[0] / jnp.where(total > 0.0, total, 1.0), 0.0)


def on_grid(x):
    return jnp.where((x >= 0) & (x < NX), jnp.float32(1.0), jnp.float32(0.0))


def brick_flags(f1_rows, f0_rows):
    low = sub_iota(8) < 4
    halves = [jnp.where(low, rows[0:1], rows[1:2]) for rows in (f1_rows, f0_rows)]
    return jnp.concatenate(halves, axis=0)


def stiffness_plane(planes, flags, x, inside_y, rwt_ref, w_ref, lane):
    num = filter_plane(planes, w_ref, lane, 1)
    inside = on_grid(x)
    rwt = rwt_ref[jnp.where(x == 0, 0, jnp.where(x == NX - 1, 2, 1))] * inside
    smooth = num * rwt
    sq = flags * (smooth * smooth)
    stiff = (inside_y * inside) * (EMIN + (sq * smooth) * (1.0 - EMIN))
    return stiff, (-3.0 * (1.0 - EMIN)) * sq * rwt


def add_moments(sums, fs, gs, outs):
    m0, m1, m2, m3 = sums
    for f, g, out in zip(fs, gs, outs):
        f, g, out = f[0:8], g[0:8], out[0:8]
        m0, m1, m2, m3 = m0 + f * f, m1 + f * g, m2 + g * g, m3 + g * out
    return m0, m1, m2, m3


def table_kernel(off_ref, _, w_ref, rwt_ref):
    store_weights(off_ref, w_ref)
    store_reciprocals(rwt_ref, w_ref, grid_y(lax.axis_index(GY)))


def inner_kernel(
    w_ref, rwt_ref, dext_ref, fext_ref, s_ref, coef_ref, g_ref, sums_ref
):
    gx, gy = lax.axis_index(GX), lax.axis_index(GY)
    lane = lane_iota(ROWS)
    iy = grid_y(gy)

    def smooth_step(p, _):
        x = p + 1
        planes = [dext_ref[p], dext_ref[p + 1], dext_ref[p + 2]]
        flags = brick_flags(fext_ref[1, x, 11:13], fext_ref[0, x, 11:13])
        s_ref[p], coef_ref[p] = stiffness_plane(
            planes, flags, gx * CX + x, iy[0], rwt_ref, w_ref, lane
        )
        return 0

    lax.fori_loop(0, CX - 2, smooth_step, 0, unroll=UNROLL[0])

    def image_step(q, _):
        outs = image_plane(
            lambda c, k: fext_ref[c, q + 2 + k], s_ref[q], s_ref[q + 1], s_ref[q + 2], lane
        )
        for c in range(3):
            g_ref[c, q] = outs[c] * iy[0]
        return 0

    lax.fori_loop(0, CX - 4, image_step, 0, unroll=UNROLL[1])

    def moment_step(t, sums):
        outs = image_plane(
            lambda c, k: g_ref[c, t + 1 + k], s_ref[t + 1], s_ref[t + 2], s_ref[t + 3], lane, 8
        )
        fs = [fext_ref[c, t + 3] for c in range(3)]
        return add_moments(sums, fs, [g_ref[c, t + 1] for c in range(3)], outs)

    zero = jnp.zeros((8, CZ), F32)
    sums = lax.fori_loop(0, CX - 6, moment_step, (zero,) * 4, unroll=UNROLL[2])
    for k in range(4):
        sums_ref[k] = sums[k]


def rim_kernel(
    second, w_in, dext_ref, fext_ref, slab_ref, s_in_ref, g_in_ref, sums_ref, rwt_ref,
    g_ref, coef_ref, f_rim_ref, mom_ref,
    d2_ref, f2_ref, s2_ref, g2_ref, w_ref, sem,
):
    w_copy = pltpu.make_async_copy(w_in, w_ref, sem)
    w_copy.start()
    gx, gy = lax.axis_index(GX), lax.axis_index(GY)
    side = partner_side(gx, second)
    lane = lane_iota(ROWS)
    iy = grid_y(gy)
    d2_ref[pl.ds(4 - 4 * side, 2)] = dext_ref[pl.ds(14 * side, 2)]
    d2_ref[pl.ds(2 * side, 4), 0:8] = slab_ref[0:4]
    d2_ref[pl.ds(2 * side, 4), 8:16] = slab_ref[13:17]
    s2_ref[pl.ds(4 - 4 * side, 3)] = s_in_ref[pl.ds(11 * side, 3)]
    for c in range(3):
        f2_ref[c, pl.ds(3 - 3 * side, 3)] = fext_ref[c, pl.ds(13 * side, 3)]
        f2_ref[c, pl.ds(3 * side, 3), 0:8] = slab_ref[4 + 3 * c : 7 + 3 * c]
        deep = slab_ref[18 + 2 * c]
        f2_ref[c, 2 + side, 8:16] = slab_ref[17 + 2 * c]
        f2_ref[c, 1 + 3 * side, 8:16] = deep
        f2_ref[c, 5 * side, 8:16] = roll(deep, -3, 0)
        f_rim_ref[c] = f2_ref[c, pl.ds(1 + 2 * side, 2)]
        g2_ref[c, pl.ds(4 - 4 * side, 2)] = g_in_ref[c, pl.ds(10 * side, 2)]
    w_copy.wait()

    def smooth_step(m, _):
        planes = [d2_ref[m + k] for k in range(3)]
        at = jnp.where(side == 0, jnp.maximum(m, 2), jnp.minimum(m + 2, 3))
        flags = brick_flags(f2_ref[1, at, 11:13], f2_ref[0, at, 11:13])
        s2_ref[m + 3 * side], coef_ref[m] = stiffness_plane(
            planes, flags, gx * CX + m - 3 + 18 * side, iy[0], rwt_ref, w_ref, lane
        )
        return 0

    lax.fori_loop(0, 4, smooth_step, 0, unroll=UNROLL[3])

    def image_step(m, _):
        n = m + side
        outs = image_plane(
            lambda c, k: f2_ref[c, m + 1 + k], s2_ref[n], s2_ref[n + 1], s2_ref[n + 2], lane
        )
        inside = iy[0] * on_grid(gx * CX + m - 2 + 16 * side)
        for c in range(3):
            g = outs[c] * inside
            g_ref[c, m] = g
            g2_ref[c, m + 2 * side] = g
        return 0

    lax.fori_loop(0, 4, image_step, 0, unroll=UNROLL[4])

    def moment_step(m, sums):
        q = m + 2 - side
        n = m + 3 - 2 * side
        outs = image_plane(
            lambda c, k: g2_ref[c, q + k], s2_ref[n - 1], s2_ref[n], s2_ref[n + 1], lane, 8
        )
        fs = [f2_ref[c, m + 3 - 3 * side] for c in range(3)]
        return add_moments(sums, fs, [g2_ref[c, q] for c in range(3)], outs)

    sums = lax.fori_loop(0, 3, moment_step, tuple(sums_ref[k] for k in range(4)), unroll=UNROLL[5])
    if not second:
        for k in range(4):
            mom_ref[k] = sums[k]
        return
    at = lax.broadcasted_iota(jnp.int32, (1, 128), 1)
    line = jnp.zeros((1, 128), F32)
    for k in range(4):
        total = jnp.sum(jnp.sum(sums[k], axis=0, keepdims=True), axis=1, keepdims=True)
        line = jnp.where(at == k, total, line)
    mom_ref[...] = line


def last_kernel(
    w_in, fext_ref, g_in_ref, coef_in_ref, g1_ref, coef1_ref, f1_ref, g2_ref, coef2_ref, f2_ref, mom_ref,
    u_hbm, sens_hbm,
    u_ref, sh_ref, coef_ref, own_ref, sens_ref, w_ref, sem,
):
    w_copy = pltpu.make_async_copy(w_in, w_ref, sem.at[3])
    w_copy.start()
    lane = lane_iota(ROWS)
    line = jnp.sum(mom_ref[...], axis=0, keepdims=True)
    at = lax.broadcasted_iota(jnp.int32, (1, 128), 1)
    m0, m1, m2, m3 = (
        jnp.sum(jnp.where(at == k, line, 0.0), axis=1, keepdims=True) for k in range(4)
    )
    inverse = 1.0 / m1
    s1 = m0 * inverse
    grow = s1 * m2 * inverse
    rr = m0 * (grow - 1.0)
    s2 = rr / (grow * grow * m1 - 2.0 * grow * s1 * m2 + s1 * s1 * m3)
    alpha = jnp.broadcast_to(s1 + s2 * grow, (ROWS, CZ))
    beta = jnp.broadcast_to(-s1 * s2, (ROWS, CZ))

    def u_plane(q, fs, gs):
        us = [alpha * f + beta * g for f, g in zip(fs, gs)]
        for c in range(3):
            u_ref[c, q] = us[c]
        return us

    def u_step(k, _):
        us = u_plane(k + 4, [fext_ref[c, k + 2] for c in range(3)], [g_in_ref[c, k] for c in range(3)])
        for c in range(3):
            own_ref[c, k + 2] = us[c][0:8]
        return 0

    lax.fori_loop(0, CX - 4, u_step, 0, unroll=4)
    coef_ref[2:16] = coef_in_ref[...]
    sides = []
    for second, rim_f_ref, g_ref, rim_ref in ((0, f1_ref, g1_ref, coef1_ref), (1, f2_ref, g2_ref, coef2_ref)):
        side = partner_side(lax.axis_index(GX), second)
        coef_ref[pl.ds(16 * side, 2)] = rim_ref[pl.ds(2 - 2 * side, 2)]
        sides.append((side, rim_f_ref, g_ref))
        for i in range(2):
            x, m = 14 * side + i, 2 - 2 * side + i
            us = u_plane(x + 2, [fext_ref[c, x] for c in range(3)], [g_ref[c, m] for c in range(3)])
            for c in range(3):
                own_ref[c, x] = us[c][0:8]
    u_copy = pltpu.make_async_copy(own_ref, u_hbm, sem.at[0])
    u_copy.start()
    for side, rim_f_ref, g_ref in sides:
        for i in range(2):
            u_plane(
                18 * side + i,
                [rim_f_ref[c, i] for c in range(3)],
                [g_ref[c, 2 * side + i] for c in range(3)],
            )

    def share_step(r, _):
        ex = ey = ez = e0 = None
        for c in range(3):
            v = u_ref[c, r + 1]
            ax, bx = v - u_ref[c, r + 2], v - u_ref[c, r]
            ay, az = v - yp(v), v - zp(v, lane)
            tx, ty, tz, t0 = ax * ax + bx * bx, ay * ay, az * az, v * v
            if c == 0:
                tx = tx + tx
            elif c == 1:
                ty = ty + ty
            else:
                tz, t0 = tz + tz, t0 + t0
            ex = tx if ex is None else ex + tx
            ey = ty if ey is None else ey + ty
            ez = tz if ez is None else ez + tz
            e0 = t0 if e0 is None else e0 + t0
        energy = 0.5 * (ex + (ey + ym(ey)) + (ez + zm(ez, lane, e0)))
        sh_ref[r] = coef_ref[r] * energy
        return 0

    lax.fori_loop(0, CX + 2, share_step, 0, unroll=UNROLL[6])

    def out_step(x, _):
        planes = [sh_ref[x], sh_ref[x + 1], sh_ref[x + 2]]
        sens_ref[x] = filter_plane(planes, w_ref, lane[0:8], -1, 8)
        return 0

    w_copy.wait()
    half = CX // 2
    copies = [u_copy]
    for k in range(2):
        lax.fori_loop(k * half, (k + 1) * half, out_step, 0, unroll=UNROLL[7])
        part = pl.ds(k * half, half)
        copies.append(pltpu.make_async_copy(sens_ref.at[part], sens_hbm.at[part], sem.at[1 + k]))
        copies[-1].start()
    for copy in copies:
        copy.wait()


VMEM = pl.BlockSpec(memory_space=pltpu.VMEM)
SMEM = pl.BlockSpec(memory_space=pltpu.SMEM)


def f32(*shape):
    return jax.ShapeDtypeStruct(shape, F32)


HBM = pl.BlockSpec(memory_space=pltpu.HBM)
ANY = pl.BlockSpec(memory_space=pl.ANY)


def call(kernel, outs, ins, out_specs, scratch, cost=None):
    return pl.pallas_call(
        kernel,
        out_shape=outs,
        in_specs=ins,
        out_specs=out_specs,
        scratch_shapes=scratch,
        cost_estimate=cost,
        compiler_params=pltpu.CompilerParams(vmem_limit_bytes=24 * 1024 * 1024),
    )


def swap(first, second, axes, count):
    got = []
    for slab, start in ((first, 1), (second, 0)):
        pairs = [(i, i + 1) for i in range(start, count - 1, 2)]
        got.append(lax.ppermute(slab, axes, pairs + [(b, a) for a, b in pairs]))
    return got


def spread_sum(line, axes, count):
    lines = jnp.broadcast_to(line, (count, 128))
    return lax.all_to_all(lines, axes, 0, 0, tiled=True)


def body(density, force, brick_ids, offsets):
    ins = (density, force, brick_ids.reshape(1, 512))
    plane = (ROWS, CZ)
    slab_y, slab_x = f32(216, CZ), f32(23, 8, CZ)
    den, f, mask, first, second = call(
        pack_y_kernel,
        (f32(CX, CY, CZ), f32(3, CX, CY, CZ), f32(8, CZ), slab_y, slab_y),
        [HBM, HBM, HBM],
        (VMEM,) * 5,
        [pltpu.VMEM((1, 512), jnp.int32), pltpu.SemaphoreType.DMA((3,))],
    )(*(pltpu.with_memory_space_constraint(a, pltpu.HBM) for a in ins))
    first, second = swap(first, second, GY, DEV_Y)
    w, rwt = call(
        table_kernel,
        (f32(128), f32(3, *plane)),
        [SMEM, ANY],
        (SMEM, VMEM),
        [],
        pl.CostEstimate(flops=1_000_000, bytes_accessed=1_000_000, transcendentals=0),
    )(pltpu.with_memory_space_constraint(offsets.T, pltpu.HBM), mask)
    dext, fext, first, second = call(
        pack_x_kernel,
        (f32(CX, *plane), f32(3, CX, *plane), slab_x, slab_x),
        [VMEM] * 5 + [ANY],
        (VMEM,) * 4,
        [],
    )(den, f, mask, first, second, w)
    first, second = swap(first, second, GX, DEV_X)
    stiff, coef, image, sums = call(
        inner_kernel,
        (f32(14, *plane), f32(14, *plane), f32(3, 12, *plane), f32(4, 8, CZ)),
        [SMEM, VMEM, VMEM, VMEM],
        (VMEM,) * 4,
        [],
        pl.CostEstimate(flops=8_000_000, bytes_accessed=8_000_000, transcendentals=0),
    )(w, rwt, dext, fext)
    rims = []
    for k, slab in enumerate((first, second)):
        image_rim, coef_rim, f_rim, sums = call(
            functools.partial(rim_kernel, k),
            (f32(3, 4, *plane), f32(4, *plane), f32(3, 2, *plane), f32(1, 128) if k else f32(4, 8, CZ)),
            [ANY] + [VMEM] * 7,
            (VMEM,) * 4,
            [
                pltpu.VMEM((6, *plane), F32),
                pltpu.VMEM((3, 6, *plane), F32),
                pltpu.VMEM((7, *plane), F32),
                pltpu.VMEM((3, 6, *plane), F32),
                pltpu.SMEM((128,), F32),
                pltpu.SemaphoreType.DMA(()),
            ],
        )(w, dext, fext, slab, stiff, image, sums, rwt)
        rims += [image_rim, coef_rim, f_rim]
    lines = spread_sum(sums, ("zl", "zh", "c"), 24)
    lines = spread_sum(jnp.sum(lines, axis=0, keepdims=True), ("x", "y"), 32)
    return call(
        last_kernel,
        (f32(3, CX, CY, CZ), f32(CX, CY, CZ)),
        [ANY] + [VMEM] * 10,
        (HBM, HBM),
        [
            pltpu.VMEM((3, CX + 4, *plane), F32),
            pltpu.VMEM((CX + 2, *plane), F32),
            pltpu.VMEM((CX + 2, *plane), F32),
            pltpu.VMEM((3, CX, CY, CZ), F32),
            pltpu.VMEM((CX, CY, CZ), F32),
            pltpu.SMEM((128,), F32),
            pltpu.SemaphoreType.DMA((4,)),
        ],
    )(w, fext, image, coef, *rims, lines)


def solution(mesh):
    fine = Mesh(mesh.devices.reshape(3, 4, 4, 8, 2), ("zl", "x", "zh", "y", "c"))
    return jax.shard_map(
        body,
        mesh=fine,
        in_specs=(P(GX, GY, None), P(None, GX, GY, None), P(GX, GY, None), P()),
        out_specs=(P(None, GX, GY, None), P(GX, GY, None)),
        check_vma=False,
    )
```

```python
import functools

import jax
import jax.numpy as jnp
import numpy as np
from jax import lax
from jax.experimental import pallas as pl
from jax.experimental.pallas import tpu as pltpu
from jax.sharding import Mesh
from jax.sharding import PartitionSpec as P

EMIN = 0.001
RADIUS = 2.0
REACH = [float(np.float32(RADIUS) - np.float32(np.sqrt(np.float32(s)))) for s in range(4)]

CX, CY, CZ = 16, 8, 256
NX, NY = 192, 512
DEV_X, DEV_Y = 12, 64
GX, GY = ("zl", "x"), ("zh", "y", "c")
ROWS = 16
F32 = jnp.float32
UNROLL = (7, 4, 5, 4, 4, 3, 9, 8)


def sub_iota(rows):
    return lax.broadcasted_iota(jnp.int32, (rows, CZ), 0)


def lane_iota(rows):
    return lax.broadcasted_iota(jnp.int32, (rows, CZ), 1)


def roll(v, shift, axis):
    return pltpu.roll(v, shift % v.shape[axis], axis)


def yp(v):
    return roll(v, -1, 0)


def ym(v):
    return roll(v, 1, 0)


def zp(v, lane, fill=0.0):
    return jnp.where(lane == CZ - 1, fill, roll(v, -1, 1))


def zm(v, lane, fill=0.0):
    return jnp.where(lane == 0, fill, roll(v, 1, 1))


def is_odd(at):
    return lax.bitwise_and(at, 1)


def partner_side(at, second):
    return 1 - is_odd(at) if second else is_odd(at)


def store_weights(off_ref, w_ref):
    for i in range(27):
        w_ref[i] = jnp.float32(0.0)
    for j in range(off_ref.shape[1]):
        dx, dy, dz = off_ref[0, j], off_ref[1, j], off_ref[2, j]
        s = dx * dx + dy * dy + dz * dz
        w = jnp.where(
            s == 0,
            jnp.float32(REACH[0]),
            jnp.where(
                s == 1,
                jnp.float32(REACH[1]),
                jnp.where(s == 2, jnp.float32(REACH[2]), jnp.float32(REACH[3])),
            ),
        )
        w_ref[(dx + 1) * 9 + (dy + 1) * 3 + dz + 1] = w


def pack_y_kernel(
    den_hbm, f_hbm, ids_hbm, den_ref, f_ref, m_ref, first_ref, second_ref, ids_ref, sem
):
    copies = [
        pltpu.make_async_copy(src, dst, sem.at[i])
        for i, (src, dst) in enumerate(((ids_hbm, ids_ref), (den_hbm, den_ref), (f_hbm, f_ref)))
    ]
    for copy in copies:
        copy.start()
    copies[0].wait()
    ids = ids_ref[...]
    row = lax.shift_right_logical(ids, 6)
    col = lax.bitwise_and(ids, 63)
    p = (lax.broadcasted_iota(jnp.int32, (8, 512), 0) == row).astype(jnp.bfloat16)
    q = (
        lax.shift_right_logical(lax.broadcasted_iota(jnp.int32, (CZ, 512), 0), 2) == col
    ).astype(jnp.bfloat16)
    flags = lax.dot_general(p, q, (((1,), (1,)), ((), ())), preferred_element_type=F32)
    m_ref[...] = flags
    copies[1].wait()
    copies[2].wait()
    den = jnp.swapaxes(den_ref[...], 0, 1)
    fs = [jnp.swapaxes(f_ref[c], 0, 1) for c in range(3)]

    odd = jnp.full((CX, CZ), is_odd(lax.axis_index(GY)), jnp.int32) == 1

    def fill(at, lo, hi):
        first_ref[at : at + 16] = jnp.where(odd, hi, lo)
        second_ref[at : at + 16] = jnp.where(odd, lo, hi)

    first_ref[208:216] = flags
    second_ref[208:216] = flags
    for j in range(4):
        fill(16 * j, den[j], den[4 + j])
    for c in range(3):
        for j in range(3):
            fill(64 + 16 * (3 * c + j), fs[c][j], fs[c][5 + j])


def pack_x_kernel(
    den_ref, f_ref, m_ref, first_in, second_in, dext_ref, fext_ref, first_ref, second_ref
):
    odd_y = jnp.full((CX, CZ), is_odd(lax.axis_index(GY)), jnp.int32) == 1

    def below(first, count):
        return jnp.where(odd_y[0:count], second_in[first : first + count], first_in[first : first + count])

    def above(first, count):
        return jnp.where(odd_y[0:count], first_in[first : first + count], second_in[first : first + count])

    def spread_flags(flags, by):
        rows = [flags[2 * bx + by : 2 * bx + by + 1] for bx in range(4)]
        return jnp.concatenate([jnp.broadcast_to(r, (4, CZ)) for r in rows], axis=0)

    def halo_rows(planes):
        return jnp.swapaxes(jnp.stack(planes), 0, 1)

    dext_ref[:, 0:8] = den_ref[...]
    dext_ref[:, 8:16] = halo_rows(
        [above(16 * j, 16) for j in range(4)] + [below(16 * j, 16) for j in range(4)]
    )
    own = m_ref[...]
    flags = (
        [spread_flags(above(208, 8), 0), spread_flags(below(208, 8), 1)],
        [spread_flags(own, 0), spread_flags(own, 1)],
        [jnp.zeros((CX, CZ), F32)] * 2,
    )
    for c in range(3):
        at = [64 + 16 * (3 * c + j) for j in range(3)]
        fext_ref[c, :, 0:8] = f_ref[c]
        fext_ref[c, :, 8:16] = halo_rows(
            [above(i, 16) for i in at] + flags[c] + [below(i, 16) for i in at]
        )
    odd_x = is_odd(lax.axis_index(GX))
    sub = sub_iota(8)
    spare = (sub == 2) | (sub == 3)
    for slab, top in ((first_ref, odd_x), (second_ref, 1 - odd_x)):
        near, deep = 13 * top, 2 + 11 * top
        slab[0:4] = dext_ref[pl.ds(12 * top, 4), 0:8]
        slab[13:17] = dext_ref[pl.ds(12 * top, 4), 8:16]
        for c in range(3):
            slab[4 + 3 * c : 7 + 3 * c] = fext_ref[c, pl.ds(near, 3), 0:8]
            slab[17 + 2 * c] = fext_ref[c, 15 * top, 8:16]
            deepest = roll(fext_ref[c, deep, 8:16], 3, 0)
            slab[18 + 2 * c] = jnp.where(spare, deepest, fext_ref[c, 1 + 13 * top, 8:16])


def filter_plane(planes, w_ref, lane, sign, rows=ROWS):
    out = None
    for dz in (-1, 0, 1):
        acc = None
        for dy in (-1, 0, 1):
            t = None
            for dx in (-1, 0, 1):
                w = w_ref[(sign * dx + 1) * 9 + (sign * dy + 1) * 3 + sign * dz + 1]
                term = planes[dx + 1][0 : rows if dy == 0 else ROWS] * w
                t = term if t is None else t + term
            if dy == 1:
                t = yp(t)
            elif dy == -1:
                t = ym(t)
            t = t[0:rows]
            acc = t if acc is None else acc + t
        if dz == 1:
            acc = zp(acc, lane)
        elif dz == -1:
            acc = zm(acc, lane)
        out = acc if out is None else out + acc
    return out


def image_plane(load, s_m, s_0, s_p, lane, rows=ROWS):
    py = 0.5 * (s_0 + yp(s_0))
    s_m, s_0, s_p, lane = s_m[0:rows], s_0[0:rows], s_p[0:rows], lane[0:rows]
    px, mx = 0.5 * (s_0 + s_p), 0.5 * (s_0 + s_m)
    pz = 0.5 * (s_0 + zp(s_0, lane))
    half = -0.5 * s_0
    outs = []
    for c in range(3):
        v = load(c, 0)
        fy = py * (v - yp(v))
        fy = fy[0:rows] - ym(fy)[0:rows]
        v = v[0:rows]
        fx = px * (v - load(c, 1)[0:rows]) + mx * (v - load(c, -1)[0:rows])
        fz = pz * (v - zp(v, lane))
        fz = fz - zm(fz, lane, half * v)
        outs.append(fx + fy + fz + (fx, fy, fz)[c])
    return outs


def grid_y(gy):
    sub = sub_iota(ROWS)
    y = jnp.where(sub < 12, sub, sub - 16) + gy * CY
    return {dy: ((y + dy >= 0) & (y + dy < NY)).astype(F32) for dy in (-1, 0, 1)}


def store_reciprocals(rwt_ref, w_ref, iy):
    lane = lane_iota(ROWS)
    iz = {dz: ((lane + dz >= 0) & (lane + dz < CZ)).astype(F32) for dz in (-1, 0, 1)}
    for case, dxs in enumerate(((0, 1), (-1, 0, 1), (-1, 0))):
        total = jnp.zeros((ROWS, CZ), F32)
        for dy in (-1, 0, 1):
            part = jnp.zeros((ROWS, CZ), F32)
            for dz in (-1, 0, 1):
                w = w_ref[(dxs[0] + 1) * 9 + (dy + 1) * 3 + dz + 1]
                for dx in dxs[1:]:
                    w = w + w_ref[(dx + 1) * 9 + (dy + 1) * 3 + dz + 1]
                part = part + w * iz[dz]
            total = total + part * iy[dy]
        rwt_ref[case] = jnp.where(total > 0.0, iy[0] / jnp.where(total > 0.0, total, 1.0), 0.0)


def on_grid(x):
    return jnp.where((x >= 0) & (x < NX), jnp.float32(1.0), jnp.float32(0.0))


def brick_flags(f1_rows, f0_rows):
    low = sub_iota(8) < 4
    halves = [jnp.where(low, rows[0:1], rows[1:2]) for rows in (f1_rows, f0_rows)]
    return jnp.concatenate(halves, axis=0)


def stiffness_plane(planes, flags, x, inside_y, rwt_ref, w_ref, lane):
    num = filter_plane(planes, w_ref, lane, 1)
    inside = on_grid(x)
    rwt = rwt_ref[jnp.where(x == 0, 0, jnp.where(x == NX - 1, 2, 1))] * inside
    smooth = num * rwt
    sq = flags * (smooth * smooth)
    stiff = (inside_y * inside) * (EMIN + (sq * smooth) * (1.0 - EMIN))
    return stiff, (-3.0 * (1.0 - EMIN)) * sq * rwt


def add_moments(sums, fs, gs, outs):
    m0, m1, m2, m3 = sums
    for f, g, out in zip(fs, gs, outs):
        f, g, out = f[0:8], g[0:8], out[0:8]
        m0, m1, m2, m3 = m0 + f * f, m1 + f * g, m2 + g * g, m3 + g * out
    return m0, m1, m2, m3


def inner_kernel(
    off_ref, dext_ref, fext_ref, w_ref, s_ref, coef_ref, g_ref, sums_ref, rwt_ref
):
    gx, gy = lax.axis_index(GX), lax.axis_index(GY)
    lane = lane_iota(ROWS)
    iy = grid_y(gy)
    store_weights(off_ref, w_ref)
    store_reciprocals(rwt_ref, w_ref, iy)

    def smooth_step(p, _):
        x = p + 1
        planes = [dext_ref[p], dext_ref[p + 1], dext_ref[p + 2]]
        flags = brick_flags(fext_ref[1, x, 11:13], fext_ref[0, x, 11:13])
        s_ref[p], coef_ref[p] = stiffness_plane(
            planes, flags, gx * CX + x, iy[0], rwt_ref, w_ref, lane
        )
        return 0

    lax.fori_loop(0, CX - 2, smooth_step, 0, unroll=UNROLL[0])

    def image_step(q, _):
        outs = image_plane(
            lambda c, k: fext_ref[c, q + 2 + k], s_ref[q], s_ref[q + 1], s_ref[q + 2], lane
        )
        for c in range(3):
            g_ref[c, q] = outs[c] * iy[0]
        return 0

    lax.fori_loop(0, CX - 4, image_step, 0, unroll=UNROLL[1])

    def moment_step(t, sums):
        outs = image_plane(
            lambda c, k: g_ref[c, t + 1 + k], s_ref[t + 1], s_ref[t + 2], s_ref[t + 3], lane, 8
        )
        fs = [fext_ref[c, t + 3] for c in range(3)]
        return add_moments(sums, fs, [g_ref[c, t + 1] for c in range(3)], outs)

    zero = jnp.zeros((8, CZ), F32)
    sums = lax.fori_loop(0, CX - 6, moment_step, (zero,) * 4, unroll=UNROLL[2])
    for k in range(4):
        sums_ref[k] = sums[k]


def rim_kernel(
    second, w_in, dext_ref, fext_ref, slab_ref, s_in_ref, g_in_ref, sums_ref, rwt_ref,
    g_ref, coef_ref, f_rim_ref, mom_ref,
    d2_ref, f2_ref, s2_ref, g2_ref, w_ref, sem,
):
    w_copy = pltpu.make_async_copy(w_in, w_ref, sem)
    w_copy.start()
    gx, gy = lax.axis_index(GX), lax.axis_index(GY)
    side = partner_side(gx, second)
    lane = lane_iota(ROWS)
    iy = grid_y(gy)
    d2_ref[pl.ds(4 - 4 * side, 2)] = dext_ref[pl.ds(14 * side, 2)]
    d2_ref[pl.ds(2 * side, 4), 0:8] = slab_ref[0:4]
    d2_ref[pl.ds(2 * side, 4), 8:16] = slab_ref[13:17]
    s2_ref[pl.ds(4 - 4 * side, 3)] = s_in_ref[pl.ds(11 * side, 3)]
    for c in range(3):
        f2_ref[c, pl.ds(3 - 3 * side, 3)] = fext_ref[c, pl.ds(13 * side, 3)]
        f2_ref[c, pl.ds(3 * side, 3), 0:8] = slab_ref[4 + 3 * c : 7 + 3 * c]
        deep = slab_ref[18 + 2 * c]
        f2_ref[c, 2 + side, 8:16] = slab_ref[17 + 2 * c]
        f2_ref[c, 1 + 3 * side, 8:16] = deep
        f2_ref[c, 5 * side, 8:16] = roll(deep, -3, 0)
        f_rim_ref[c] = f2_ref[c, pl.ds(1 + 2 * side, 2)]
        g2_ref[c, pl.ds(4 - 4 * side, 2)] = g_in_ref[c, pl.ds(10 * side, 2)]
    w_copy.wait()

    def smooth_step(m, _):
        planes = [d2_ref[m + k] for k in range(3)]
        at = jnp.where(side == 0, jnp.maximum(m, 2), jnp.minimum(m + 2, 3))
        flags = brick_flags(f2_ref[1, at, 11:13], f2_ref[0, at, 11:13])
        s2_ref[m + 3 * side], coef_ref[m] = stiffness_plane(
            planes, flags, gx * CX + m - 3 + 18 * side, iy[0], rwt_ref, w_ref, lane
        )
        return 0

    lax.fori_loop(0, 4, smooth_step, 0, unroll=UNROLL[3])

    def image_step(m, _):
        n = m + side
        outs = image_plane(
            lambda c, k: f2_ref[c, m + 1 + k], s2_ref[n], s2_ref[n + 1], s2_ref[n + 2], lane
        )
        inside = iy[0] * on_grid(gx * CX + m - 2 + 16 * side)
        for c in range(3):
            g = outs[c] * inside
            g_ref[c, m] = g
            g2_ref[c, m + 2 * side] = g
        return 0

    lax.fori_loop(0, 4, image_step, 0, unroll=UNROLL[4])

    def moment_step(m, sums):
        q = m + 2 - side
        n = m + 3 - 2 * side
        outs = image_plane(
            lambda c, k: g2_ref[c, q + k], s2_ref[n - 1], s2_ref[n], s2_ref[n + 1], lane, 8
        )
        fs = [f2_ref[c, m + 3 - 3 * side] for c in range(3)]
        return add_moments(sums, fs, [g2_ref[c, q] for c in range(3)], outs)

    sums = lax.fori_loop(0, 3, moment_step, tuple(sums_ref[k] for k in range(4)), unroll=UNROLL[5])
    if not second:
        for k in range(4):
            mom_ref[k] = sums[k]
        return
    at = lax.broadcasted_iota(jnp.int32, (1, 128), 1)
    line = jnp.zeros((1, 128), F32)
    for k in range(4):
        total = jnp.sum(jnp.sum(sums[k], axis=0, keepdims=True), axis=1, keepdims=True)
        line = jnp.where(at == k, total, line)
    mom_ref[...] = line


def last_kernel(
    w_in, fext_ref, g_in_ref, coef_in_ref, g1_ref, coef1_ref, f1_ref, g2_ref, coef2_ref, f2_ref, mom_ref,
    u_hbm, sens_hbm,
    u_ref, sh_ref, coef_ref, own_ref, sens_ref, w_ref, sem,
):
    w_copy = pltpu.make_async_copy(w_in, w_ref, sem.at[3])
    w_copy.start()
    lane = lane_iota(ROWS)
    line = jnp.sum(mom_ref[...], axis=0, keepdims=True)
    at = lax.broadcasted_iota(jnp.int32, (1, 128), 1)
    m0, m1, m2, m3 = (
        jnp.sum(jnp.where(at == k, line, 0.0), axis=1, keepdims=True) for k in range(4)
    )
    inverse = 1.0 / m1
    s1 = m0 * inverse
    grow = s1 * m2 * inverse
    rr = m0 * (grow - 1.0)
    s2 = rr / (grow * grow * m1 - 2.0 * grow * s1 * m2 + s1 * s1 * m3)
    alpha = jnp.broadcast_to(s1 + s2 * grow, (ROWS, CZ))
    beta = jnp.broadcast_to(-s1 * s2, (ROWS, CZ))

    def u_plane(q, fs, gs):
        us = [alpha * f + beta * g for f, g in zip(fs, gs)]
        for c in range(3):
            u_ref[c, q] = us[c]
        return us

    def u_step(k, _):
        us = u_plane(k + 4, [fext_ref[c, k + 2] for c in range(3)], [g_in_ref[c, k] for c in range(3)])
        for c in range(3):
            own_ref[c, k + 2] = us[c][0:8]
        return 0

    lax.fori_loop(0, CX - 4, u_step, 0, unroll=4)
    coef_ref[2:16] = coef_in_ref[...]
    sides = []
    for second, rim_f_ref, g_ref, rim_ref in ((0, f1_ref, g1_ref, coef1_ref), (1, f2_ref, g2_ref, coef2_ref)):
        side = partner_side(lax.axis_index(GX), second)
        coef_ref[pl.ds(16 * side, 2)] = rim_ref[pl.ds(2 - 2 * side, 2)]
        sides.append((side, rim_f_ref, g_ref))
        for i in range(2):
            x, m = 14 * side + i, 2 - 2 * side + i
            us = u_plane(x + 2, [fext_ref[c, x] for c in range(3)], [g_ref[c, m] for c in range(3)])
            for c in range(3):
                own_ref[c, x] = us[c][0:8]
    u_copy = pltpu.make_async_copy(own_ref, u_hbm, sem.at[0])
    u_copy.start()
    for side, rim_f_ref, g_ref in sides:
        for i in range(2):
            u_plane(
                18 * side + i,
                [rim_f_ref[c, i] for c in range(3)],
                [g_ref[c, 2 * side + i] for c in range(3)],
            )

    def share_step(r, _):
        ex = ey = ez = e0 = None
        for c in range(3):
            v = u_ref[c, r + 1]
            ax, bx = v - u_ref[c, r + 2], v - u_ref[c, r]
            ay, az = v - yp(v), v - zp(v, lane)
            tx, ty, tz, t0 = ax * ax + bx * bx, ay * ay, az * az, v * v
            if c == 0:
                tx = tx + tx
            elif c == 1:
                ty = ty + ty
            else:
                tz, t0 = tz + tz, t0 + t0
            ex = tx if ex is None else ex + tx
            ey = ty if ey is None else ey + ty
            ez = tz if ez is None else ez + tz
            e0 = t0 if e0 is None else e0 + t0
        energy = 0.5 * (ex + (ey + ym(ey)) + (ez + zm(ez, lane, e0)))
        sh_ref[r] = coef_ref[r] * energy
        return 0

    lax.fori_loop(0, CX + 2, share_step, 0, unroll=UNROLL[6])

    def out_step(x, _):
        planes = [sh_ref[x], sh_ref[x + 1], sh_ref[x + 2]]
        sens_ref[x] = filter_plane(planes, w_ref, lane[0:8], -1, 8)
        return 0

    w_copy.wait()
    half = CX // 2
    copies = [u_copy]
    for k in range(2):
        lax.fori_loop(k * half, (k + 1) * half, out_step, 0, unroll=UNROLL[7])
        part = pl.ds(k * half, half)
        copies.append(pltpu.make_async_copy(sens_ref.at[part], sens_hbm.at[part], sem.at[1 + k]))
        copies[-1].start()
    for copy in copies:
        copy.wait()


VMEM = pl.BlockSpec(memory_space=pltpu.VMEM)
SMEM = pl.BlockSpec(memory_space=pltpu.SMEM)


def f32(*shape):
    return jax.ShapeDtypeStruct(shape, F32)


HBM = pl.BlockSpec(memory_space=pltpu.HBM)
ANY = pl.BlockSpec(memory_space=pl.ANY)


def call(kernel, outs, ins, out_specs, scratch, cost=None):
    return pl.pallas_call(
        kernel,
        out_shape=outs,
        in_specs=ins,
        out_specs=out_specs,
        scratch_shapes=scratch,
        cost_estimate=cost,
        compiler_params=pltpu.CompilerParams(vmem_limit_bytes=24 * 1024 * 1024),
    )


def swap(first, second, axes, count):
    got = []
    for slab, start in ((first, 1), (second, 0)):
        pairs = [(i, i + 1) for i in range(start, count - 1, 2)]
        got.append(lax.ppermute(slab, axes, pairs + [(b, a) for a, b in pairs]))
    return got


def spread_sum(line, axes, count):
    lines = jnp.broadcast_to(line, (count, 128))
    return lax.all_to_all(lines, axes, 0, 0, tiled=True)


def body(density, force, brick_ids, offsets):
    ins = (density, force, brick_ids.reshape(1, 512))
    plane = (ROWS, CZ)
    slab_y, slab_x = f32(216, CZ), f32(23, 8, CZ)
    den, f, mask, first, second = call(
        pack_y_kernel,
        (f32(CX, CY, CZ), f32(3, CX, CY, CZ), f32(8, CZ), slab_y, slab_y),
        [HBM, HBM, HBM],
        (VMEM,) * 5,
        [pltpu.VMEM((1, 512), jnp.int32), pltpu.SemaphoreType.DMA((3,))],
    )(*(pltpu.with_memory_space_constraint(a, pltpu.HBM) for a in ins))
    first, second = swap(first, second, GY, DEV_Y)
    dext, fext, first, second = call(
        pack_x_kernel,
        (f32(CX, *plane), f32(3, CX, *plane), slab_x, slab_x),
        [VMEM] * 5,
        (VMEM,) * 4,
        [],
    )(den, f, mask, first, second)
    first, second = swap(first, second, GX, DEV_X)
    w, stiff, coef, image, sums, rwt = call(
        inner_kernel,
        (f32(128), f32(14, *plane), f32(14, *plane), f32(3, 12, *plane), f32(4, 8, CZ), f32(3, *plane)),
        [SMEM, VMEM, VMEM],
        (SMEM,) + (VMEM,) * 5,
        [],
        pl.CostEstimate(flops=8_000_000, bytes_accessed=8_000_000, transcendentals=0),
    )(pltpu.with_memory_space_constraint(offsets.T, pltpu.HBM), dext, fext)
    rims = []
    for k, slab in enumerate((first, second)):
        image_rim, coef_rim, f_rim, sums = call(
            functools.partial(rim_kernel, k),
            (f32(3, 4, *plane), f32(4, *plane), f32(3, 2, *plane), f32(1, 128) if k else f32(4, 8, CZ)),
            [ANY] + [VMEM] * 7,
            (VMEM,) * 4,
            [
                pltpu.VMEM((6, *plane), F32),
                pltpu.VMEM((3, 6, *plane), F32),
                pltpu.VMEM((7, *plane), F32),
                pltpu.VMEM((3, 6, *plane), F32),
                pltpu.SMEM((128,), F32),
                pltpu.SemaphoreType.DMA(()),
            ],
        )(w, dext, fext, slab, stiff, image, sums, rwt)
        rims += [image_rim, coef_rim, f_rim]
    lines = spread_sum(sums, ("zl", "zh", "c"), 24)
    lines = spread_sum(jnp.sum(lines, axis=0, keepdims=True), ("x", "y"), 32)
    return call(
        last_kernel,
        (f32(3, CX, CY, CZ), f32(CX, CY, CZ)),
        [ANY] + [VMEM] * 10,
        (HBM, HBM),
        [
            pltpu.VMEM((3, CX + 4, *plane), F32),
            pltpu.VMEM((CX + 2, *plane), F32),
            pltpu.VMEM((CX + 2, *plane), F32),
            pltpu.VMEM((3, CX, CY, CZ), F32),
            pltpu.VMEM((CX, CY, CZ), F32),
            pltpu.SMEM((128,), F32),
            pltpu.SemaphoreType.DMA((4,)),
        ],
    )(w, fext, image, coef, *rims, lines)


def solution(mesh):
    fine = Mesh(mesh.devices.reshape(3, 4, 4, 8, 2), ("zl", "x", "zh", "y", "c"))
    return jax.shard_map(
        body,
        mesh=fine,
        in_specs=(P(GX, GY, None), P(None, GX, GY, None), P(GX, GY, None), P()),
        out_specs=(P(None, GX, GY, None), P(GX, GY, None)),
        check_vma=False,
    )
```
